32 devices in a mesh: panel: 4 (over y, x), leaf: 8 (over z, core).
Axes of the slice: x: 2, y: 2, z: 4, core: 2. Of those that a mesh axis runs over, the one named last changes fastest.
Arguments:
- excitation: bfloat16 [2, 128, 98304], P(None, None, ('panel', 'leaf')), may hold values from -6 to 6
- point_order: int32 [32, 3072], P(('panel', 'leaf')), may hold values from 0 to 3071, each once within a row
- projection: bfloat16 [2, 256, 98304], P(None, None, ('panel', 'leaf')), may hold values from -0.078125 to 0.078125
- transfer: bfloat16 [3, 2, 8192, 512], P(None, None, ('panel', 'leaf')), may hold values from -0.1875 to 0.1875
- expansion: bfloat16 [2, 256, 98304], P(None, None, ('panel', 'leaf')), may hold values from -0.125 to 0.125
Outputs:
- response: bfloat16 [2, 128, 98304], P(None, None, ('panel', 'leaf'))
The draws below stay inside these ranges and needn't reach their ends.
Inputs may be any that keep to these rules, and one draw needn't show every extreme that they name: Each row of point_order holds every number of 0 to 3071 once.
All inputs are finite; a program needn't handle non-finite values.
Results may differ from the reference program's by a relative error of at most 0.018.
Values may be sent and summed in bfloat16 or wider, within the bound.
A program may use at most 64 MiB of HBM per device.

```python
import jax
import jax.numpy as jnp
from jax import lax

R = 256
EXC = 128
ROWS = 3072
LEVELS = 3
N = 98304
N_PANEL = 4
N_LEAF = 8


def shard_levels(key, extent, shards, low, top_value):
    level = 1.0
    for axis_at, parts in shards:
        steps = jax.random.uniform(jax.random.fold_in(jax.random.fold_in(key, 6), axis_at), (parts,), jnp.float32, low / len(shards), top_value / len(shards))
        level = level * jnp.repeat(jnp.exp(steps), extent[axis_at] // parts).reshape((-1,) + (1,) * (len(extent) - 1 - axis_at))
    return level


def bell_draw(rng, dims, spread, bound, split=(), held_as=jnp.bfloat16):
    drawn = spread * jax.random.normal(rng, dims, jnp.float32)
    if split:
        drawn = drawn * shard_levels(rng, dims, split, -0.22, 0.18)
    return jnp.clip(drawn, -bound, bound).astype(held_as)


def setup_inputs(seed: int = 0) -> dict:
    key_of = jax.random.split(jax.random.key(seed), 6)
    excitation = bell_draw(key_of[0], (2, EXC, N), 1.0, 6.0, ((2, 32),))
    point_order = jax.vmap(lambda own: jax.random.permutation(own, ROWS))(jax.random.split(key_of[1], (N_PANEL * N_LEAF))).reshape((N_PANEL * N_LEAF, ROWS)).astype(jnp.int32)
    projection = bell_draw(key_of[2], (2, R, N), (2 * ROWS) ** -0.5, 0.078125, ((2, 32),))
    transfer = bell_draw(key_of[3], (LEVELS, 2, N_PANEL * N_LEAF * R, 2 * R), (4 * R) ** -0.5, 0.1875, ((2, 32),))
    expansion = bell_draw(key_of[4], (2, R, N), (2 * R * N_PANEL) ** -0.5, 0.125, ((2, 32),))
    return dict(excitation=excitation, point_order=point_order, projection=projection, transfer=transfer, expansion=expansion)


def complex_dot(first_matrix, second_matrix, first_dim, second_dim):
    contract = (((first_dim,), (second_dim,)), ((), ()))

    def real_dot(first_part, second_part):
        return lax.dot_general(first_part, second_part, contract, preferred_element_type=jnp.float32)

    real_part = real_dot(first_matrix[0], second_matrix[0]) - real_dot(first_matrix[1], second_matrix[1])
    imag_part = real_dot(first_matrix[0], second_matrix[1]) + real_dot(first_matrix[1], second_matrix[0])
    return jnp.stack((real_part, imag_part))


def complex_einsum(form, first_matrix, second_matrix):
    first_wide = first_matrix.astype(jnp.float32)
    second_wide = second_matrix.astype(jnp.float32)
    real_part = jnp.einsum(form, first_wide[0], second_wide[0]) - jnp.einsum(form, first_wide[1], second_wide[1])
    imag_part = jnp.einsum(form, first_wide[0], second_wide[1]) + jnp.einsum(form, first_wide[1], second_wide[0])
    return jnp.stack((real_part, imag_part))


def reference(excitation, point_order, projection, transfer, expansion):
    node_count = N_PANEL * N_LEAF
    reshaped = excitation.reshape(2, EXC, node_count, ROWS)

    def project(block_index):
        block_values = lax.dynamic_index_in_dim(reshaped, block_index, 2, keepdims=False)
        order_row = lax.dynamic_index_in_dim(point_order, block_index, 0, keepdims=False)
        ordered = jnp.take(block_values, order_row, axis=2)
        basis = lax.dynamic_slice_in_dim(projection, (block_index * ROWS).astype(jnp.int32), ROWS, 2)
        return complex_dot(basis, ordered, 1, 1).astype(jnp.bfloat16)

    blocks_coeff = lax.map(project, jnp.arange(node_count, dtype=jnp.int32))
    coefficients = jnp.transpose(blocks_coeff, (1, 0, 2, 3)).reshape(2, N_PANEL, N_LEAF, R, EXC)
    for level in range(LEVELS):
        span = 2 ** level
        grouped = coefficients.reshape(2, N_PANEL, N_LEAF // (2 * span), 2, span, R, EXC)
        lower_side = jnp.broadcast_to(grouped[:, :, :, 0:1], grouped.shape).reshape(coefficients.shape)
        upper_side = jnp.broadcast_to(grouped[:, :, :, 1:2], grouped.shape).reshape(coefficients.shape)
        matrices = transfer[level].reshape(2, N_PANEL, N_LEAF, R, 2 * R)
        mixed_sum = complex_einsum("pnrk,pnke->pnre", matrices[..., :R], lower_side)
        mixed_sum = mixed_sum + complex_einsum("pnrk,pnke->pnre", matrices[..., R:], upper_side)
        coefficients = mixed_sum.astype(jnp.bfloat16)
    total = jnp.sum(coefficients.astype(jnp.float32), axis=1).astype(jnp.bfloat16)

    def expand(panel_index):
        start_col = (panel_index * N_LEAF * ROWS).astype(jnp.int32)
        basis = lax.dynamic_slice_in_dim(expansion, start_col, N_LEAF * ROWS, 2).reshape(2, R, N_LEAF, ROWS)
        return complex_einsum("ike,kir->eir", total, basis)

    expanded = lax.map(expand, jnp.arange(N_PANEL, dtype=jnp.int32))
    response = jnp.transpose(expanded, (1, 2, 0, 3, 4)).reshape(2, EXC, N)
    return response.astype(jnp.bfloat16)
```

```python
import functools

import jax
import jax.numpy as jnp
from jax import lax
from jax.experimental import pallas as pl
from jax.experimental.pallas import tpu as pltpu
from jax.sharding import PartitionSpec as P

MESH = pl.DeviceIdType.MESH
CHUNKS = 2
MIB = 1 << 20


def tile_of(extent, most, unit=128):
    tile = most
    while extent % tile or tile % unit:
        tile -= unit
    return tile


def combine(product, rank, width):
    real = product[:rank, :width] - product[rank:, width:]
    imag = product[:rank, width:] + product[rank:, :width]
    return jnp.concatenate((real, imag), axis=1).astype(jnp.bfloat16)


def coefficients_kernel(
    panels, leaves, levels,
    excitation_hbm, order_ref, projection_hbm, transfer_hbm, out_ref,
    excitation, projection, transfer, points, order_wide, level_zero, held, arrived, scattered, total,
    load_sem, level_send, level_recv, scatter_send, scatter_recv, gather_send, gather_recv,
):
    panel = lax.axis_index("panel")
    leaf = lax.axis_index("leaf")
    _, exc, rows = excitation.shape
    rank = projection.shape[1]
    part = exc // CHUNKS
    wide = 2 * part

    loads = [
        pltpu.make_async_copy(excitation_hbm, excitation, load_sem.at[0]),
        pltpu.make_async_copy(projection_hbm, projection, load_sem.at[1]),
        pltpu.make_async_copy(transfer_hbm, transfer, load_sem.at[2]),
    ]
    for load in loads:
        load.start()

    partners, bits = [], []
    for level in range(levels):
        span = 1 << level
        bit = lax.rem(lax.div(leaf, span), 2)
        bits.append(bit)
        partners.append(leaf + span - 2 * span * bit)
    peers = [lax.rem(panel + step, panels) for step in range(1, panels)]

    barrier = pltpu.get_barrier_semaphore()
    for partner in partners:
        pl.semaphore_signal(barrier, inc=1, device_id=(panel, partner), device_id_type=MESH)
    for peer in peers:
        pl.semaphore_signal(barrier, inc=1, device_id=(peer, leaf), device_id_type=MESH)

    for start in range(0, rows, 128):
        row = order_ref[:, start:start + 128]
        order_wide[start:start + 128, :] = jnp.broadcast_to(row, (128, 128)).T.astype(jnp.int16)

    loads[0].wait()
    source_tile = tile_of(rows, 512)
    for start in range(0, rows, source_tile):
        for chunk in range(CHUNKS):
            lanes = slice(chunk * part, (chunk + 1) * part)
            both = jnp.concatenate(
                (excitation[0, lanes, start:start + source_tile], excitation[1, lanes, start:start + source_tile]), axis=0
            )
            points[start:start + source_tile, chunk * wide:(chunk + 1) * wide] = both.T

    loads[1].wait()
    level_zero[...] = jnp.zeros_like(level_zero)
    tile = tile_of(rows, 512)

    def gather_and_project(step, carry):
        begin = pl.multiple_of(step * tile, tile)
        wanted = order_wide[pl.ds(begin, tile), :]
        lane = lax.broadcasted_iota(jnp.int32, (tile, 128), 1).astype(jnp.int16)
        one = jnp.ones((tile, 128), jnp.bfloat16)
        zero = jnp.zeros((tile, 128), jnp.bfloat16)
        chosen = jnp.concatenate(
            [jnp.where(wanted == lane + jnp.int16(start), one, zero) for start in range(0, rows, 128)], axis=1
        )
        ordered = jnp.dot(chosen, points[...], preferred_element_type=jnp.float32).astype(jnp.bfloat16)
        for side in range(2):
            level_zero[side * rank:(side + 1) * rank, :] += jnp.dot(
                projection[side, :, pl.ds(begin, tile)], ordered, preferred_element_type=jnp.float32
            )
        return carry

    lax.fori_loop(0, rows // tile, gather_and_project, 0)

    pl.semaphore_wait(barrier, levels + panels - 1)
    loads[2].wait()

    def level_copy(level, chunk):
        return pltpu.make_async_remote_copy(
            src_ref=held.at[level, chunk],
            dst_ref=arrived.at[level, chunk],
            send_sem=level_send.at[level, chunk],
            recv_sem=level_recv.at[level, chunk],
            device_id=(panel, partners[level]),
            device_id_type=MESH,
        )

    piece = rank // panels

    def scatter_copy(step, chunk):
        return pltpu.make_async_remote_copy(
            src_ref=held.at[levels, chunk, pl.ds(pl.multiple_of(peers[step] * piece, piece), piece)],
            dst_ref=scattered.at[step, chunk],
            send_sem=scatter_send.at[step, chunk],
            recv_sem=scatter_recv.at[step, chunk],
            device_id=(peers[step], leaf),
            device_id_type=MESH,
        )

    mine = pl.ds(pl.multiple_of(panel * piece, piece), piece)

    def gather_copy(step, chunk):
        return pltpu.make_async_remote_copy(
            src_ref=total.at[chunk, mine],
            dst_ref=total.at[chunk, mine],
            send_sem=gather_send.at[step, chunk],
            recv_sem=gather_recv.at[step, chunk],
            device_id=(peers[step], leaf),
            device_id_type=MESH,
        )

    def send_on(level, chunk):
        if level < levels:
            level_copy(level, chunk).start()
        else:
            for step in range(panels - 1):
                scatter_copy(step, chunk).start()

    for chunk in range(CHUNKS):
        held[0, chunk] = combine(level_zero[:, chunk * wide:(chunk + 1) * wide], rank, part)
        send_on(0, chunk)
    for level in range(levels):
        own_at = pl.ds(pl.multiple_of(bits[level] * rank, rank), rank)
        other_at = pl.ds(pl.multiple_of((1 - bits[level]) * rank, rank), rank)
        own = [
            jnp.dot(
                transfer[level, :, :, own_at].reshape(2 * rank, rank), held[level, chunk],
                preferred_element_type=jnp.float32,
            )
            for chunk in range(CHUNKS)
        ]
        for chunk in range(CHUNKS):
            level_copy(level, chunk).wait_recv()
            other = jnp.dot(
                transfer[level, :, :, other_at].reshape(2 * rank, rank), arrived[level, chunk],
                preferred_element_type=jnp.float32,
            )
            held[level + 1, chunk] = combine(own[chunk] + other, rank, part)
            send_on(level + 1, chunk)
    for chunk in range(CHUNKS):
        summed = held[levels, chunk, mine].astype(jnp.float32)
        for step in range(panels - 1):
            scatter_copy(step, chunk).wait_recv()
            summed = summed + scattered[step, chunk].astype(jnp.float32)
        total[chunk, mine] = summed.astype(jnp.bfloat16)
        for step in range(panels - 1):
            gather_copy(step, chunk).start()
    for chunk in range(CHUNKS):
        for step in range(panels - 1):
            gather_copy(step, chunk).wait_recv()
        turned = total[chunk].T
        for side in range(2):
            at = side * exc + chunk * part
            out_ref[at:at + part, :] = turned[side * part:(side + 1) * part]
    for chunk in range(CHUNKS):
        for level in range(levels):
            level_copy(level, chunk).wait_send()
        for step in range(panels - 1):
            scatter_copy(step, chunk).wait_send()
            gather_copy(step, chunk).wait_send()


def expansion_kernel(total_ref, expansion_ref, out_ref):
    exc = total_ref.shape[0] // 2
    first = jnp.dot(total_ref[...], expansion_ref[0], preferred_element_type=jnp.float32)
    second = jnp.dot(total_ref[...], expansion_ref[1], preferred_element_type=jnp.float32)
    out_ref[0] = (first[:exc] - second[exc:]).astype(out_ref.dtype)
    out_ref[1] = (second[:exc] + first[exc:]).astype(out_ref.dtype)


def per_device(excitation, point_order, projection, transfer, expansion):
    panels = lax.axis_size("panel")
    leaves = lax.axis_size("leaf")
    levels = transfer.shape[0]
    _, exc, rows = excitation.shape
    rank = projection.shape[1]
    wide = 2 * exc // CHUNKS
    total = pl.pallas_call(
        functools.partial(coefficients_kernel, panels, leaves, levels),
        out_shape=jax.ShapeDtypeStruct((2 * exc, rank), jnp.bfloat16),
        in_specs=[
            pl.BlockSpec(memory_space=pl.ANY),
            pl.BlockSpec(memory_space=pltpu.VMEM),
            pl.BlockSpec(memory_space=pl.ANY),
            pl.BlockSpec(memory_space=pl.ANY),
        ],
        out_specs=pl.BlockSpec(memory_space=pltpu.VMEM),
        scratch_shapes=[
            pltpu.VMEM(excitation.shape, jnp.bfloat16),
            pltpu.VMEM(projection.shape, jnp.bfloat16),
            pltpu.VMEM(transfer.shape, jnp.bfloat16),
            pltpu.VMEM((rows, 2 * exc), jnp.bfloat16),
            pltpu.VMEM((rows, 128), jnp.int16),
            pltpu.VMEM((2 * rank, 2 * exc), jnp.float32),
            pltpu.VMEM((levels + 1, CHUNKS, rank, wide), jnp.bfloat16),
            pltpu.VMEM((levels, CHUNKS, rank, wide), jnp.bfloat16),
            pltpu.VMEM((panels - 1, CHUNKS, rank // panels, wide), jnp.bfloat16),
            pltpu.VMEM((CHUNKS, rank, wide), jnp.bfloat16),
            pltpu.SemaphoreType.DMA((3,)),
            pltpu.SemaphoreType.DMA((levels, CHUNKS)),
            pltpu.SemaphoreType.DMA((levels, CHUNKS)),
            pltpu.SemaphoreType.DMA((panels - 1, CHUNKS)),
            pltpu.SemaphoreType.DMA((panels - 1, CHUNKS)),
            pltpu.SemaphoreType.DMA((panels - 1, CHUNKS)),
            pltpu.SemaphoreType.DMA((panels - 1, CHUNKS)),
        ],
        compiler_params=pltpu.CompilerParams(
            collective_id=0, has_side_effects=True, vmem_limit_bytes=32 * MIB
        ),
    )(excitation, point_order, projection, transfer)
    columns = tile_of(rows, 1024)
    return pl.pallas_call(
        expansion_kernel,
        out_shape=jax.ShapeDtypeStruct((2, exc, rows), jnp.bfloat16),
        grid=(rows // columns,),
        in_specs=[
            pl.BlockSpec((2 * exc, rank), lambda step: (0, 0)),
            pl.BlockSpec((2, rank, columns), lambda step: (0, 0, step)),
        ],
        out_specs=pl.BlockSpec((2, exc, columns), lambda step: (0, 0, step)),
        compiler_params=pltpu.CompilerParams(vmem_limit_bytes=16 * MIB),
    )(total, expansion)


def solution(mesh):
    in_specs = (
        P(None, None, ("panel", "leaf")),
        P(("panel", "leaf"), None),
        P(None, None, ("panel", "leaf")),
        P(None, None, ("panel", "leaf"), None),
        P(None, None, ("panel", "leaf")),
    )
    out_specs = P(None, None, ("panel", "leaf"))
    return jax.shard_map(
        per_device, mesh=mesh, in_specs=in_specs, out_specs=out_specs, check_vma=False
    )
```

```python
import functools

import jax
import jax.numpy as jnp
from jax import lax
from jax.experimental import pallas as pl
from jax.experimental.pallas import tpu as pltpu
from jax.sharding import PartitionSpec as P

MESH = pl.DeviceIdType.MESH
CHUNKS = 2
MIB = 1 << 20


def tile_of(extent, most, unit=128):
    tile = most
    while extent % tile or tile % unit:
        tile -= unit
    return tile


def combine(product, rank, width):
    real = product[:rank, :width] - product[rank:, width:]
    imag = product[:rank, width:] + product[rank:, :width]
    return jnp.concatenate((real, imag), axis=1).astype(jnp.bfloat16)


def projection_kernel(
    excitation_hbm, order_hbm, projection_hbm, out_ref,
    excitation, order, projection, points, order_wide, level_zero, load_sem,
):
    _, exc, rows = excitation_hbm.shape
    rank = projection.shape[1]
    part = exc // CHUNKS
    wide = 2 * part
    loads = [pltpu.make_async_copy(order_hbm, order, load_sem.at[0])]
    for chunk in range(CHUNKS):
        for side in range(2):
            at = chunk * wide + side * part
            loads.append(
                pltpu.make_async_copy(
                    excitation_hbm.at[side, pl.ds(chunk * part, part)], excitation.at[pl.ds(at, part)],
                    load_sem.at[1 + 2 * chunk + side],
                )
            )
    loads.append(pltpu.make_async_copy(projection_hbm, projection, load_sem.at[1 + 2 * CHUNKS]))
    for load in loads:
        load.start()

    loads[0].wait()
    for start in range(0, rows, 128):
        row = order[:, start:start + 128]
        order_wide[start:start + 128, :] = jnp.broadcast_to(row, (128, 128)).T.astype(jnp.int16)

    for load in loads[1:-1]:
        load.wait()
    source_tile = tile_of(rows, 512)
    for start in range(0, rows, source_tile):
        points[start:start + source_tile, :] = excitation[:, start:start + source_tile].T

    loads[-1].wait()
    level_zero[...] = jnp.zeros_like(level_zero)
    tile = tile_of(rows, 1024)

    def gather_and_project(step, carry):
        begin = pl.multiple_of(step * tile, tile)
        wanted = order_wide[pl.ds(begin, tile), :]
        lane = lax.broadcasted_iota(jnp.int32, (tile, 128), 1).astype(jnp.int16)
        one = jnp.ones((tile, 128), jnp.bfloat16)
        zero = jnp.zeros((tile, 128), jnp.bfloat16)
        chosen = jnp.concatenate(
            [jnp.where(wanted == lane + jnp.int16(start), one, zero) for start in range(0, rows, 128)], axis=1
        )
        ordered = jnp.dot(chosen, points[...], preferred_element_type=jnp.float32).astype(jnp.bfloat16)
        for side in range(2):
            level_zero[side * rank:(side + 1) * rank, :] += jnp.dot(
                projection[side, :, pl.ds(begin, tile)], ordered, preferred_element_type=jnp.float32
            )
        return carry

    lax.fori_loop(0, rows // tile, gather_and_project, 0)
    for chunk in range(CHUNKS):
        out_ref[chunk] = combine(level_zero[:, chunk * wide:(chunk + 1) * wide], rank, part)


def butterfly_kernel(
    panels, levels, exc,
    start_ref, transfer_hbm, out_ref,
    transfer, held, arrived, scattered, total,
    load_sem, level_send, level_recv, scatter_send, scatter_recv, gather_send, gather_recv,
):
    panel = lax.axis_index("panel")
    leaf = lax.axis_index("leaf")
    rank = start_ref.shape[1]
    part = exc // CHUNKS

    load = pltpu.make_async_copy(transfer_hbm, transfer, load_sem)
    load.start()
    partners, bits = [], []
    for level in range(levels):
        span = 1 << level
        bit = lax.rem(lax.div(leaf, span), 2)
        bits.append(bit)
        partners.append(leaf + span - 2 * span * bit)
    peers = [lax.rem(panel + step, panels) for step in range(1, panels)]

    barrier = pltpu.get_barrier_semaphore()
    for partner in partners:
        pl.semaphore_signal(barrier, inc=1, device_id=(panel, partner), device_id_type=MESH)
    for peer in peers:
        pl.semaphore_signal(barrier, inc=1, device_id=(peer, leaf), device_id_type=MESH)
    pl.semaphore_wait(barrier, levels + panels - 1)

    def level_copy(level, chunk):
        return pltpu.make_async_remote_copy(
            src_ref=held.at[level, chunk],
            dst_ref=arrived.at[level, chunk],
            send_sem=level_send.at[level, chunk],
            recv_sem=level_recv.at[level, chunk],
            device_id=(panel, partners[level]),
            device_id_type=MESH,
        )

    piece = rank // panels

    def scatter_copy(step, chunk):
        return pltpu.make_async_remote_copy(
            src_ref=held.at[levels, chunk, pl.ds(pl.multiple_of(peers[step] * piece, piece), piece)],
            dst_ref=scattered.at[step, chunk],
            send_sem=scatter_send.at[step, chunk],
            recv_sem=scatter_recv.at[step, chunk],
            device_id=(peers[step], leaf),
            device_id_type=MESH,
        )

    mine = pl.ds(pl.multiple_of(panel * piece, piece), piece)

    def gather_copy(step, chunk):
        return pltpu.make_async_remote_copy(
            src_ref=total.at[chunk, mine],
            dst_ref=total.at[chunk, mine],
            send_sem=gather_send.at[step, chunk],
            recv_sem=gather_recv.at[step, chunk],
            device_id=(peers[step], leaf),
            device_id_type=MESH,
        )

    def send_on(level, chunk):
        if level < levels:
            level_copy(level, chunk).start()
        else:
            for step in range(panels - 1):
                scatter_copy(step, chunk).start()

    for chunk in range(CHUNKS):
        held[0, chunk] = start_ref[chunk]
        send_on(0, chunk)
    load.wait()
    for level in range(levels):
        own_at = pl.ds(pl.multiple_of(bits[level] * rank, rank), rank)
        other_at = pl.ds(pl.multiple_of((1 - bits[level]) * rank, rank), rank)
        own = [
            jnp.dot(
                transfer[level, :, :, own_at].reshape(2 * rank, rank), held[level, chunk],
                preferred_element_type=jnp.float32,
            )
            for chunk in range(CHUNKS)
        ]
        for chunk in range(CHUNKS):
            level_copy(level, chunk).wait_recv()
            other = jnp.dot(
                transfer[level, :, :, other_at].reshape(2 * rank, rank), arrived[level, chunk],
                preferred_element_type=jnp.float32,
            )
            held[level + 1, chunk] = combine(own[chunk] + other, rank, part)
            send_on(level + 1, chunk)
    for chunk in range(CHUNKS):
        summed = held[levels, chunk, mine].astype(jnp.float32)
        for step in range(panels - 1):
            scatter_copy(step, chunk).wait_recv()
            summed = summed + scattered[step, chunk].astype(jnp.float32)
        total[chunk, mine] = summed.astype(jnp.bfloat16)
        for step in range(panels - 1):
            gather_copy(step, chunk).start()
    for chunk in range(CHUNKS):
        for step in range(panels - 1):
            gather_copy(step, chunk).wait_recv()
        turned = total[chunk].T
        for side in range(2):
            at = side * exc + chunk * part
            out_ref[at:at + part, :] = turned[side * part:(side + 1) * part]
    for chunk in range(CHUNKS):
        for level in range(levels):
            level_copy(level, chunk).wait_send()
        for step in range(panels - 1):
            scatter_copy(step, chunk).wait_send()
            gather_copy(step, chunk).wait_send()


def expansion_kernel(total_ref, expansion_ref, out_ref):
    exc = total_ref.shape[0] // 2
    first = jnp.dot(total_ref[...], expansion_ref[0], preferred_element_type=jnp.float32)
    second = jnp.dot(total_ref[...], expansion_ref[1], preferred_element_type=jnp.float32)
    out_ref[0] = (first[:exc] - second[exc:]).astype(out_ref.dtype)
    out_ref[1] = (second[:exc] + first[exc:]).astype(out_ref.dtype)


def per_device(excitation, point_order, projection, transfer, expansion):
    panels = lax.axis_size("panel")
    levels = transfer.shape[0]
    _, exc, rows = excitation.shape
    rank = projection.shape[1]
    wide = 2 * exc // CHUNKS
    level_zero = pl.pallas_call(
        projection_kernel,
        out_shape=jax.ShapeDtypeStruct((CHUNKS, rank, wide), jnp.bfloat16),
        in_specs=[pl.BlockSpec(memory_space=pltpu.HBM)] * 3,
        out_specs=pl.BlockSpec(memory_space=pltpu.VMEM),
        scratch_shapes=[
            pltpu.VMEM((2 * exc, rows), jnp.bfloat16),
            pltpu.VMEM((1, rows), jnp.int32),
            pltpu.VMEM(projection.shape, jnp.bfloat16),
            pltpu.VMEM((rows, 2 * exc), jnp.bfloat16),
            pltpu.VMEM((rows, 128), jnp.int16),
            pltpu.VMEM((2 * rank, 2 * exc), jnp.float32),
            pltpu.SemaphoreType.DMA((2 + 2 * CHUNKS,)),
        ],
        compiler_params=pltpu.CompilerParams(vmem_limit_bytes=60 * MIB),
    )(excitation, point_order, projection)
    total = pl.pallas_call(
        functools.partial(butterfly_kernel, panels, levels, exc),
        out_shape=jax.ShapeDtypeStruct((2 * exc, rank), jnp.bfloat16),
        in_specs=[pl.BlockSpec(memory_space=pltpu.VMEM), pl.BlockSpec(memory_space=pltpu.HBM)],
        out_specs=pl.BlockSpec(memory_space=pltpu.VMEM),
        scratch_shapes=[
            pltpu.VMEM(transfer.shape, jnp.bfloat16),
            pltpu.VMEM((levels + 1, CHUNKS, rank, wide), jnp.bfloat16),
            pltpu.VMEM((levels, CHUNKS, rank, wide), jnp.bfloat16),
            pltpu.VMEM((panels - 1, CHUNKS, rank // panels, wide), jnp.bfloat16),
            pltpu.VMEM((CHUNKS, rank, wide), jnp.bfloat16),
            pltpu.SemaphoreType.DMA,
            pltpu.SemaphoreType.DMA((levels, CHUNKS)),
            pltpu.SemaphoreType.DMA((levels, CHUNKS)),
            pltpu.SemaphoreType.DMA((panels - 1, CHUNKS)),
            pltpu.SemaphoreType.DMA((panels - 1, CHUNKS)),
            pltpu.SemaphoreType.DMA((panels - 1, CHUNKS)),
            pltpu.SemaphoreType.DMA((panels - 1, CHUNKS)),
        ],
        compiler_params=pltpu.CompilerParams(
            collective_id=0, has_side_effects=True, vmem_limit_bytes=24 * MIB
        ),
    )(level_zero, transfer)
    columns = tile_of(rows, 1024)
    return pl.pallas_call(
        expansion_kernel,
        out_shape=jax.ShapeDtypeStruct((2, exc, rows), jnp.bfloat16),
        grid=(rows // columns,),
        in_specs=[
            pl.BlockSpec((2 * exc, rank), lambda step: (0, 0)),
            pl.BlockSpec((2, rank, columns), lambda step: (0, 0, step)),
        ],
        out_specs=pl.BlockSpec((2, exc, columns), lambda step: (0, 0, step)),
        compiler_params=pltpu.CompilerParams(vmem_limit_bytes=16 * MIB),
    )(total, expansion)


def solution(mesh):
    in_specs = (
        P(None, None, ("panel", "leaf")),
        P(("panel", "leaf"), None),
        P(None, None, ("panel", "leaf")),
        P(None, None, ("panel", "leaf"), None),
        P(None, None, ("panel", "leaf")),
    )
    out_specs = P(None, None, ("panel", "leaf"))
    return jax.shard_map(
        per_device, mesh=mesh, in_specs=in_specs, out_specs=out_specs, check_vma=False
    )
```

```python
import functools

import jax
import jax.numpy as jnp
from jax import lax
from jax.experimental import pallas as pl
from jax.experimental.pallas import tpu as pltpu
from jax.sharding import PartitionSpec as P

MESH = pl.DeviceIdType.MESH
CHUNKS = 2
MIB = 1 << 20


def tile_of(extent, most, unit=128):
    tile = most
    while extent % tile or tile % unit:
        tile -= unit
    return tile


def combine(product, rank, width):
    real = product[:rank, :width] - product[rank:, width:]
    imag = product[:rank, width:] + product[rank:, :width]
    return jnp.concatenate((real, imag), axis=1).astype(jnp.bfloat16)


def coefficients_kernel(
    panels, levels,
    excitation_hbm, order_hbm, projection_hbm, transfer_hbm, out_ref,
    excitation, order, projection, transfer, crossing, points, order_wide, ordered,
    held, arrived, partial, scattered, cross_out, cross_in, total,
    load_sem, matrix_sem, level_send, level_recv, scatter_send, scatter_recv,
    cross_send, cross_recv, gather_send, gather_recv,
):
    panel = lax.axis_index("panel")
    leaf = lax.axis_index("leaf")
    _, exc, rows = excitation_hbm.shape
    rank = projection.shape[1]
    part = exc // CHUNKS
    wide = 2 * part
    top = levels - 1

    loads = [pltpu.make_async_copy(order_hbm, order, load_sem.at[0])]
    for chunk in range(CHUNKS):
        for side in range(2):
            at = chunk * wide + side * part
            loads.append(
                pltpu.make_async_copy(
                    excitation_hbm.at[side, pl.ds(chunk * part, part)], excitation.at[pl.ds(at, part)],
                    load_sem.at[3 + 2 * chunk + side],
                )
            )
    projection_load = pltpu.make_async_copy(projection_hbm, projection, load_sem.at[1])
    transfer_load = pltpu.make_async_copy(transfer_hbm, transfer, load_sem.at[2])
    for load in loads:
        load.start()
    projection_load.start()
    transfer_load.start()

    partners, bits = [], []
    for level in range(levels):
        span = 1 << level
        bit = lax.rem(lax.div(leaf, span), 2)
        bits.append(bit)
        partners.append(leaf + span - 2 * span * bit)
    peers = [lax.rem(panel + step, panels) for step in range(1, panels)]
    own_at = [pl.ds(pl.multiple_of(bit * rank, rank), rank) for bit in bits]
    other_at = [pl.ds(pl.multiple_of((1 - bit) * rank, rank), rank) for bit in bits]

    barrier = pltpu.get_barrier_semaphore()
    for partner in partners:
        pl.semaphore_signal(barrier, inc=1, device_id=(panel, partner), device_id_type=MESH)
    for peer in peers:
        pl.semaphore_signal(barrier, inc=1, device_id=(peer, leaf), device_id_type=MESH)

    loads[0].wait()
    for start in range(0, rows, 128):
        row = order[:, start:start + 128]
        order_wide[start:start + 128, :] = jnp.broadcast_to(row, (128, 128)).T.astype(jnp.int16)
    for load in loads[1:]:
        load.wait()

    pl.semaphore_wait(barrier, levels + panels - 1)
    matrix_copy = pltpu.make_async_remote_copy(
        src_ref=transfer_hbm.at[top, :, :, other_at[top]],
        dst_ref=crossing,
        send_sem=matrix_sem.at[0],
        recv_sem=matrix_sem.at[1],
        device_id=(panel, partners[top]),
        device_id_type=MESH,
    )
    matrix_copy.start()

    source_tile = tile_of(rows, 512)
    for start in range(0, rows, source_tile):
        points[start:start + source_tile, :] = excitation[:, start:start + source_tile].T

    tile = tile_of(rows, 512)
    lane = lax.broadcasted_iota(jnp.int32, (tile, 128), 1).astype(jnp.int16)
    one = jnp.ones((tile, 128), jnp.bfloat16)
    zero = jnp.zeros((tile, 128), jnp.bfloat16)
    for begin in range(0, rows, tile):
        wanted = order_wide[begin:begin + tile, :]
        chosen = jnp.concatenate(
            [jnp.where(wanted == lane + jnp.int16(start), one, zero) for start in range(0, rows, 128)], axis=1
        )
        ordered[begin:begin + tile, :] = jnp.dot(
            chosen, points[...], preferred_element_type=jnp.float32
        ).astype(jnp.bfloat16)

    projection_load.wait()
    level_zero = jnp.dot(
        projection[...].reshape(2 * rank, rows), ordered[...], preferred_element_type=jnp.float32
    )

    def level_copy(level, chunk):
        return pltpu.make_async_remote_copy(
            src_ref=held.at[level, chunk],
            dst_ref=arrived.at[level, chunk],
            send_sem=level_send.at[level, chunk],
            recv_sem=level_recv.at[level, chunk],
            device_id=(panel, partners[level]),
            device_id_type=MESH,
        )

    piece = rank // panels

    def scatter_copy(step, chunk):
        return pltpu.make_async_remote_copy(
            src_ref=partial.at[chunk, :, pl.ds(pl.multiple_of(peers[step] * piece, piece), piece)],
            dst_ref=scattered.at[step, chunk],
            send_sem=scatter_send.at[step, chunk],
            recv_sem=scatter_recv.at[step, chunk],
            device_id=(peers[step], leaf),
            device_id_type=MESH,
        )

    def cross_copy(chunk):
        return pltpu.make_async_remote_copy(
            src_ref=cross_out.at[chunk],
            dst_ref=cross_in.at[chunk],
            send_sem=cross_send.at[chunk],
            recv_sem=cross_recv.at[chunk],
            device_id=(panel, partners[top]),
            device_id_type=MESH,
        )

    mine = pl.ds(pl.multiple_of(panel * piece, piece), piece)

    def gather_copy(step, chunk):
        return pltpu.make_async_remote_copy(
            src_ref=total.at[chunk, mine],
            dst_ref=total.at[chunk, mine],
            send_sem=gather_send.at[step, chunk],
            recv_sem=gather_recv.at[step, chunk],
            device_id=(peers[step], leaf),
            device_id_type=MESH,
        )

    def product(matrix, block):
        return jnp.dot(matrix.reshape(2 * rank, rank), block, preferred_element_type=jnp.float32)

    for chunk in range(CHUNKS):
        held[0, chunk] = combine(level_zero[:, chunk * wide:(chunk + 1) * wide], rank, part)
        if top > 0:
            level_copy(0, chunk).start()
    transfer_load.wait()
    for level in range(top):
        own = [product(transfer[level, :, :, own_at[level]], held[level, chunk]) for chunk in range(CHUNKS)]
        for chunk in range(CHUNKS):
            level_copy(level, chunk).wait_recv()
            other = product(transfer[level, :, :, other_at[level]], arrived[level, chunk])
            held[level + 1, chunk] = combine(own[chunk] + other, rank, part)
            if level + 1 < top:
                level_copy(level + 1, chunk).start()
            else:
                if chunk == 0:
                    matrix_copy.wait_recv()
                partial[chunk, 0] = combine(
                    product(transfer[top, :, :, own_at[top]], held[top, chunk]), rank, part
                )
                partial[chunk, 1] = combine(product(crossing[...], held[top, chunk]), rank, part)
                for step in range(panels - 1):
                    scatter_copy(step, chunk).start()
    kept = []
    for chunk in range(CHUNKS):
        sums = [partial[chunk, side, mine].astype(jnp.float32) for side in range(2)]
        for step in range(panels - 1):
            scatter_copy(step, chunk).wait_recv()
            sums = [sums[side] + scattered[step, chunk, side].astype(jnp.float32) for side in range(2)]
        cross_out[chunk] = sums[1].astype(jnp.bfloat16)
        cross_copy(chunk).start()
        kept.append(sums[0])
    for chunk in range(CHUNKS):
        cross_copy(chunk).wait_recv()
        total[chunk, mine] = (kept[chunk] + cross_in[chunk].astype(jnp.float32)).astype(jnp.bfloat16)
        for step in range(panels - 1):
            gather_copy(step, chunk).start()
    for chunk in range(CHUNKS):
        for step in range(panels - 1):
            gather_copy(step, chunk).wait_recv()
        turned = total[chunk].T
        for side in range(2):
            at = side * exc + chunk * part
            out_ref[at:at + part, :] = turned[side * part:(side + 1) * part]
    matrix_copy.wait_send()
    for chunk in range(CHUNKS):
        for level in range(top):
            level_copy(level, chunk).wait_send()
        cross_copy(chunk).wait_send()
        for step in range(panels - 1):
            scatter_copy(step, chunk).wait_send()
            gather_copy(step, chunk).wait_send()


def expansion_kernel(total_hbm, expansion_ref, out_hbm, total_ref, out, load_sem, store_sem):
    load = pltpu.make_async_copy(total_hbm, total_ref, load_sem)
    load.start()
    load.wait()
    exc = total_ref.shape[0] // 2
    rows = expansion_ref.shape[2]
    columns = tile_of(rows, 768)
    stores = []
    for step in range(rows // columns):
        span = slice(step * columns, (step + 1) * columns)
        first = jnp.dot(total_ref[...], expansion_ref[0, :, span], preferred_element_type=jnp.float32)
        second = jnp.dot(total_ref[...], expansion_ref[1, :, span], preferred_element_type=jnp.float32)
        out[0, :, span] = (first[:exc] - second[exc:]).astype(out.dtype)
        out[1, :, span] = (second[:exc] + first[exc:]).astype(out.dtype)
        at = pl.ds(step * columns, columns)
        store = pltpu.make_async_copy(out.at[:, :, at], out_hbm.at[:, :, at], store_sem.at[step])
        store.start()
        stores.append(store)
    for store in stores:
        store.wait()


def per_device(excitation, point_order, projection, transfer, expansion):
    panels = lax.axis_size("panel")
    levels = transfer.shape[0]
    _, exc, rows = excitation.shape
    rank = projection.shape[1]
    wide = 2 * exc // CHUNKS
    piece = rank // panels
    total = pl.pallas_call(
        functools.partial(coefficients_kernel, panels, levels),
        out_shape=jax.ShapeDtypeStruct((2 * exc, rank), jnp.bfloat16),
        in_specs=[pl.BlockSpec(memory_space=pl.ANY)] * 4,
        out_specs=pl.BlockSpec(memory_space=pltpu.VMEM),
        scratch_shapes=[
            pltpu.VMEM((2 * exc, rows), jnp.bfloat16),
            pltpu.VMEM((1, rows), jnp.int32),
            pltpu.VMEM(projection.shape, jnp.bfloat16),
            pltpu.VMEM(transfer.shape, jnp.bfloat16),
            pltpu.VMEM((2, rank, rank), jnp.bfloat16),
            pltpu.VMEM((rows, 2 * exc), jnp.bfloat16),
            pltpu.VMEM((rows, 128), jnp.int16),
            pltpu.VMEM((rows, 2 * exc), jnp.bfloat16),
            pltpu.VMEM((levels, CHUNKS, rank, wide), jnp.bfloat16),
            pltpu.VMEM((levels, CHUNKS, rank, wide), jnp.bfloat16),
            pltpu.VMEM((CHUNKS, 2, rank, wide), jnp.bfloat16),
            pltpu.VMEM((panels - 1, CHUNKS, 2, piece, wide), jnp.bfloat16),
            pltpu.VMEM((CHUNKS, piece, wide), jnp.bfloat16),
            pltpu.VMEM((CHUNKS, piece, wide), jnp.bfloat16),
            pltpu.VMEM((CHUNKS, rank, wide), jnp.bfloat16),
            pltpu.SemaphoreType.DMA((3 + 2 * CHUNKS,)),
            pltpu.SemaphoreType.DMA((2,)),
            pltpu.SemaphoreType.DMA((levels, CHUNKS)),
            pltpu.SemaphoreType.DMA((levels, CHUNKS)),
            pltpu.SemaphoreType.DMA((panels - 1, CHUNKS)),
            pltpu.SemaphoreType.DMA((panels - 1, CHUNKS)),
            pltpu.SemaphoreType.DMA((CHUNKS,)),
            pltpu.SemaphoreType.DMA((CHUNKS,)),
            pltpu.SemaphoreType.DMA((panels - 1, CHUNKS)),
            pltpu.SemaphoreType.DMA((panels - 1, CHUNKS)),
        ],
        compiler_params=pltpu.CompilerParams(
            collective_id=0, has_side_effects=True, vmem_limit_bytes=60 * MIB
        ),
    )(excitation, point_order, projection, transfer)
    return pl.pallas_call(
        expansion_kernel,
        out_shape=jax.ShapeDtypeStruct((2, exc, rows), jnp.bfloat16),
        in_specs=[pl.BlockSpec(memory_space=pl.ANY), pl.BlockSpec(memory_space=pltpu.VMEM)],
        out_specs=pl.BlockSpec(memory_space=pl.ANY),
        scratch_shapes=[
            pltpu.VMEM((2 * exc, rank), jnp.bfloat16),
            pltpu.VMEM((2, exc, rows), jnp.bfloat16),
            pltpu.SemaphoreType.DMA,
            pltpu.SemaphoreType.DMA((rows // tile_of(rows, 768),)),
        ],
        compiler_params=pltpu.CompilerParams(vmem_limit_bytes=60 * MIB),
    )(total, expansion)


def solution(mesh):
    in_specs = (
        P(None, None, ("panel", "leaf")),
        P(("panel", "leaf"), None),
        P(None, None, ("panel", "leaf")),
        P(None, None, ("panel", "leaf"), None),
        P(None, None, ("panel", "leaf")),
    )
    out_specs = P(None, None, ("panel", "leaf"))
    return jax.shard_map(
        per_device, mesh=mesh, in_specs=in_specs, out_specs=out_specs, check_vma=False
    )
```

```python
import functools

import jax
import jax.numpy as jnp
from jax import lax
from jax.experimental import pallas as pl
from jax.experimental.pallas import tpu as pltpu
from jax.sharding import PartitionSpec as P

MESH = pl.DeviceIdType.MESH
CHUNKS = 2
GROUP = 16
MIB = 1 << 20


def tile_of(extent, most, unit=128):
    tile = most
    while extent % tile or tile % unit:
        tile -= unit
    return tile


def combine(product, rank, width):
    real = product[:rank, :width] - product[rank:, width:]
    imag = product[:rank, width:] + product[rank:, :width]
    return jnp.concatenate((real, imag), axis=1).astype(jnp.bfloat16)


def coefficients_kernel(
    panels, levels,
    excitation_hbm, order_hbm, projection_hbm, transfer_hbm, out_ref,
    excitation, order, order_scalar, projection, transfer, crossing, points, points_wide, picked, order_wide, ordered,
    held, arrived, partial, scattered, cross_out, cross_in, total,
    load_sem, matrix_sem, level_send, level_recv, scatter_send, scatter_recv,
    cross_send, cross_recv, gather_send, gather_recv,
):
    panel = lax.axis_index("panel")
    leaf = lax.axis_index("leaf")
    _, exc, rows = excitation_hbm.shape
    rank = projection.shape[1]
    part = exc // CHUNKS
    wide = 2 * part
    top = levels - 1

    loads = [pltpu.make_async_copy(order_hbm, order, load_sem.at[0])]
    for chunk in range(CHUNKS):
        for side in range(2):
            at = chunk * wide + side * part
            loads.append(
                pltpu.make_async_copy(
                    excitation_hbm.at[side, pl.ds(chunk * part, part)], excitation.at[pl.ds(at, part)],
                    load_sem.at[3 + 2 * chunk + side],
                )
            )
    scalar_load = pltpu.make_async_copy(order_hbm, order_scalar, load_sem.at[3 + 2 * CHUNKS])
    projection_load = pltpu.make_async_copy(projection_hbm, projection, load_sem.at[1])
    transfer_load = pltpu.make_async_copy(transfer_hbm, transfer, load_sem.at[2])
    for load in loads:
        load.start()
    scalar_load.start()
    projection_load.start()
    transfer_load.start()

    partners, bits = [], []
    for level in range(levels):
        span = 1 << level
        bit = lax.rem(lax.div(leaf, span), 2)
        bits.append(bit)
        partners.append(leaf + span - 2 * span * bit)
    peers = [lax.rem(panel + step, panels) for step in range(1, panels)]
    own_at = [pl.ds(pl.multiple_of(bit * rank, rank), rank) for bit in bits]
    other_at = [pl.ds(pl.multiple_of((1 - bit) * rank, rank), rank) for bit in bits]

    barrier = pltpu.get_barrier_semaphore()
    for partner in partners:
        pl.semaphore_signal(barrier, inc=1, device_id=(panel, partner), device_id_type=MESH)
    for peer in peers:
        pl.semaphore_signal(barrier, inc=1, device_id=(peer, leaf), device_id_type=MESH)

    loads[0].wait()
    for start in range(0, rows, 128):
        row = order[:, start:start + 128]
        order_wide[start:start + 128, :] = jnp.broadcast_to(row, (128, 128)).T.astype(jnp.int16)
    for load in loads[1:]:
        load.wait()

    pl.semaphore_wait(barrier, levels + panels - 1)
    matrix_copy = pltpu.make_async_remote_copy(
        src_ref=transfer_hbm.at[top, :, :, other_at[top]],
        dst_ref=crossing,
        send_sem=matrix_sem.at[0],
        recv_sem=matrix_sem.at[1],
        device_id=(panel, partners[top]),
        device_id_type=MESH,
    )
    matrix_copy.start()

    source_tile = tile_of(rows, 512)
    for start in range(0, rows, source_tile):
        turned = excitation[:, start:start + source_tile].T
        points[start:start + source_tile, :] = turned
        points_wide[start:start + source_tile, :] = turned.astype(jnp.float32)
    scalar_load.wait()

    tile = tile_of(rows, 512)
    read = picked.shape[0]

    def gather(step, carry):
        begin = pl.multiple_of(step * tile, tile)
        for base in range(0, read, GROUP):
            found = [
                points_wide[pl.ds(order_scalar[0, begin + base + row], 1), :] for row in range(GROUP)
            ]
            for row in range(GROUP):
                picked[base + row:base + row + 1, :] = found[row]
        wanted = order_wide[pl.ds(begin + read, tile - read), :]
        lane = lax.broadcasted_iota(jnp.int32, wanted.shape, 1).astype(jnp.int16)
        one = jnp.ones(wanted.shape, jnp.bfloat16)
        zero = jnp.zeros(wanted.shape, jnp.bfloat16)
        chosen = jnp.concatenate(
            [jnp.where(wanted == lane + jnp.int16(start), one, zero) for start in range(0, rows, 128)], axis=1
        )
        ordered[pl.ds(begin + read, tile - read), :] = jnp.dot(
            chosen, points[...], preferred_element_type=jnp.float32
        ).astype(jnp.bfloat16)
        ordered[pl.ds(begin, read), :] = picked[...].astype(jnp.bfloat16)
        return carry

    lax.fori_loop(0, rows // tile, gather, 0)

    projection_load.wait()
    level_zero = jnp.dot(
        projection[...].reshape(2 * rank, rows), ordered[...], preferred_element_type=jnp.float32
    )

    def level_copy(level, chunk):
        return pltpu.make_async_remote_copy(
            src_ref=held.at[level, chunk],
            dst_ref=arrived.at[level, chunk],
            send_sem=level_send.at[level, chunk],
            recv_sem=level_recv.at[level, chunk],
            device_id=(panel, partners[level]),
            device_id_type=MESH,
        )

    piece = rank // panels

    def scatter_copy(step, chunk):
        return pltpu.make_async_remote_copy(
            src_ref=partial.at[chunk, :, pl.ds(pl.multiple_of(peers[step] * piece, piece), piece)],
            dst_ref=scattered.at[step, chunk],
            send_sem=scatter_send.at[step, chunk],
            recv_sem=scatter_recv.at[step, chunk],
            device_id=(peers[step], leaf),
            device_id_type=MESH,
        )

    def cross_copy(chunk):
        return pltpu.make_async_remote_copy(
            src_ref=cross_out.at[chunk],
            dst_ref=cross_in.at[chunk],
            send_sem=cross_send.at[chunk],
            recv_sem=cross_recv.at[chunk],
            device_id=(panel, partners[top]),
            device_id_type=MESH,
        )

    mine = pl.ds(pl.multiple_of(panel * piece, piece), piece)

    def gather_copy(step, chunk):
        return pltpu.make_async_remote_copy(
            src_ref=total.at[chunk, mine],
            dst_ref=total.at[chunk, mine],
            send_sem=gather_send.at[step, chunk],
            recv_sem=gather_recv.at[step, chunk],
            device_id=(peers[step], leaf),
            device_id_type=MESH,
        )

    def product(matrix, block):
        return jnp.dot(matrix.reshape(2 * rank, rank), block, preferred_element_type=jnp.float32)

    for chunk in range(CHUNKS):
        held[0, chunk] = combine(level_zero[:, chunk * wide:(chunk + 1) * wide], rank, part)
        if top > 0:
            level_copy(0, chunk).start()
    transfer_load.wait()
    for level in range(top):
        own = [product(transfer[level, :, :, own_at[level]], held[level, chunk]) for chunk in range(CHUNKS)]
        for chunk in range(CHUNKS):
            level_copy(level, chunk).wait_recv()
            other = product(transfer[level, :, :, other_at[level]], arrived[level, chunk])
            held[level + 1, chunk] = combine(own[chunk] + other, rank, part)
            if level + 1 < top:
                level_copy(level + 1, chunk).start()
            else:
                if chunk == 0:
                    matrix_copy.wait_recv()
                partial[chunk, 0] = combine(
                    product(transfer[top, :, :, own_at[top]], held[top, chunk]), rank, part
                )
                partial[chunk, 1] = combine(product(crossing[...], held[top, chunk]), rank, part)
                for step in range(panels - 1):
                    scatter_copy(step, chunk).start()
    kept = []
    for chunk in range(CHUNKS):
        sums = [partial[chunk, side, mine].astype(jnp.float32) for side in range(2)]
        for step in range(panels - 1):
            scatter_copy(step, chunk).wait_recv()
            sums = [sums[side] + scattered[step, chunk, side].astype(jnp.float32) for side in range(2)]
        cross_out[chunk] = sums[1].astype(jnp.bfloat16)
        cross_copy(chunk).start()
        kept.append(sums[0])
    for chunk in range(CHUNKS):
        cross_copy(chunk).wait_recv()
        total[chunk, mine] = (kept[chunk] + cross_in[chunk].astype(jnp.float32)).astype(jnp.bfloat16)
        for step in range(panels - 1):
            gather_copy(step, chunk).start()
    for chunk in range(CHUNKS):
        for step in range(panels - 1):
            gather_copy(step, chunk).wait_recv()
        turned = total[chunk].T
        for side in range(2):
            at = side * exc + chunk * part
            out_ref[at:at + part, :] = turned[side * part:(side + 1) * part]
    matrix_copy.wait_send()
    for chunk in range(CHUNKS):
        for level in range(top):
            level_copy(level, chunk).wait_send()
        cross_copy(chunk).wait_send()
        for step in range(panels - 1):
            scatter_copy(step, chunk).wait_send()
            gather_copy(step, chunk).wait_send()


def expansion_kernel(total_hbm, expansion_ref, out_hbm, total_ref, out, load_sem, store_sem):
    load = pltpu.make_async_copy(total_hbm, total_ref, load_sem)
    load.start()
    load.wait()
    exc = total_ref.shape[0] // 2
    rows = expansion_ref.shape[2]
    columns = tile_of(rows, 768)
    stores = []
    for step in range(rows // columns):
        span = slice(step * columns, (step + 1) * columns)
        first = jnp.dot(total_ref[...], expansion_ref[0, :, span], preferred_element_type=jnp.float32)
        second = jnp.dot(total_ref[...], expansion_ref[1, :, span], preferred_element_type=jnp.float32)
        out[0, :, span] = (first[:exc] - second[exc:]).astype(out.dtype)
        out[1, :, span] = (second[:exc] + first[exc:]).astype(out.dtype)
        at = pl.ds(step * columns, columns)
        store = pltpu.make_async_copy(out.at[:, :, at], out_hbm.at[:, :, at], store_sem.at[step])
        store.start()
        stores.append(store)
    for store in stores:
        store.wait()


def per_device(excitation, point_order, projection, transfer, expansion):
    panels = lax.axis_size("panel")
    levels = transfer.shape[0]
    _, exc, rows = excitation.shape
    rank = projection.shape[1]
    wide = 2 * exc // CHUNKS
    piece = rank // panels
    total = pl.pallas_call(
        functools.partial(coefficients_kernel, panels, levels),
        out_shape=jax.ShapeDtypeStruct((2 * exc, rank), jnp.bfloat16),
        in_specs=[pl.BlockSpec(memory_space=pl.ANY)] * 4,
        out_specs=pl.BlockSpec(memory_space=pltpu.VMEM),
        scratch_shapes=[
            pltpu.VMEM((2 * exc, rows), jnp.bfloat16),
            pltpu.VMEM((1, rows), jnp.int32),
            pltpu.SMEM((1, rows), jnp.int32),
            pltpu.VMEM(projection.shape, jnp.bfloat16),
            pltpu.VMEM(transfer.shape, jnp.bfloat16),
            pltpu.VMEM((2, rank, rank), jnp.bfloat16),
            pltpu.VMEM((rows, 2 * exc), jnp.bfloat16),
            pltpu.VMEM((rows, 2 * exc), jnp.float32),
            pltpu.VMEM((tile_of(rows, 512) // 2, 2 * exc), jnp.float32),
            pltpu.VMEM((rows, 128), jnp.int16),
            pltpu.VMEM((rows, 2 * exc), jnp.bfloat16),
            pltpu.VMEM((levels, CHUNKS, rank, wide), jnp.bfloat16),
            pltpu.VMEM((levels, CHUNKS, rank, wide), jnp.bfloat16),
            pltpu.VMEM((CHUNKS, 2, rank, wide), jnp.bfloat16),
            pltpu.VMEM((panels - 1, CHUNKS, 2, piece, wide), jnp.bfloat16),
            pltpu.VMEM((CHUNKS, piece, wide), jnp.bfloat16),
            pltpu.VMEM((CHUNKS, piece, wide), jnp.bfloat16),
            pltpu.VMEM((CHUNKS, rank, wide), jnp.bfloat16),
            pltpu.SemaphoreType.DMA((4 + 2 * CHUNKS,)),
            pltpu.SemaphoreType.DMA((2,)),
            pltpu.SemaphoreType.DMA((levels, CHUNKS)),
            pltpu.SemaphoreType.DMA((levels, CHUNKS)),
            pltpu.SemaphoreType.DMA((panels - 1, CHUNKS)),
            pltpu.SemaphoreType.DMA((panels - 1, CHUNKS)),
            pltpu.SemaphoreType.DMA((CHUNKS,)),
            pltpu.SemaphoreType.DMA((CHUNKS,)),
            pltpu.SemaphoreType.DMA((panels - 1, CHUNKS)),
            pltpu.SemaphoreType.DMA((panels - 1, CHUNKS)),
        ],
        compiler_params=pltpu.CompilerParams(
            collective_id=0, has_side_effects=True, vmem_limit_bytes=60 * MIB
        ),
    )(excitation, point_order, projection, transfer)
    return pl.pallas_call(
        expansion_kernel,
        out_shape=jax.ShapeDtypeStruct((2, exc, rows), jnp.bfloat16),
        in_specs=[pl.BlockSpec(memory_space=pl.ANY), pl.BlockSpec(memory_space=pltpu.VMEM)],
        out_specs=pl.BlockSpec(memory_space=pl.ANY),
        scratch_shapes=[
            pltpu.VMEM((2 * exc, rank), jnp.bfloat16),
            pltpu.VMEM((2, exc, rows), jnp.bfloat16),
            pltpu.SemaphoreType.DMA,
            pltpu.SemaphoreType.DMA((rows // tile_of(rows, 768),)),
        ],
        compiler_params=pltpu.CompilerParams(vmem_limit_bytes=24 * MIB),
    )(total, expansion)


def solution(mesh):
    in_specs = (
        P(None, None, ("panel", "leaf")),
        P(("panel", "leaf"), None),
        P(None, None, ("panel", "leaf")),
        P(None, None, ("panel", "leaf"), None),
        P(None, None, ("panel", "leaf")),
    )
    out_specs = P(None, None, ("panel", "leaf"))
    return jax.shard_map(
        per_device, mesh=mesh, in_specs=in_specs, out_specs=out_specs, check_vma=False
    )
```

```python
import functools

import jax
import jax.numpy as jnp
from jax import lax
from jax.experimental import pallas as pl
from jax.experimental.pallas import tpu as pltpu
from jax.sharding import PartitionSpec as P

MESH = pl.DeviceIdType.MESH
CHUNKS = 1
GROUP = 16
MIB = 1 << 20


def tile_of(extent, most, unit=128):
    tile = most
    while extent % tile or tile % unit:
        tile -= unit
    return tile


def combine(product, rank, width):
    real = product[:rank, :width] - product[rank:, width:]
    imag = product[:rank, width:] + product[rank:, :width]
    return jnp.concatenate((real, imag), axis=1).astype(jnp.bfloat16)


def coefficients_kernel(
    panels, levels,
    excitation_hbm, order_hbm, projection_hbm, transfer_hbm, out_ref,
    excitation, order, order_scalar, projection, transfer, crossing, points, points_wide, picked, order_wide, ordered,
    held, arrived, partial, scattered, cross_out, cross_in, total,
    load_sem, matrix_sem, level_send, level_recv, scatter_send, scatter_recv,
    cross_send, cross_recv, gather_send, gather_recv,
):
    panel = lax.axis_index("panel")
    leaf = lax.axis_index("leaf")
    _, exc, rows = excitation_hbm.shape
    rank = projection.shape[1]
    part = exc // CHUNKS
    wide = 2 * part
    top = levels - 1

    loads = [pltpu.make_async_copy(order_hbm, order, load_sem.at[0])]
    for chunk in range(CHUNKS):
        for side in range(2):
            at = chunk * wide + side * part
            loads.append(
                pltpu.make_async_copy(
                    excitation_hbm.at[side, pl.ds(chunk * part, part)], excitation.at[pl.ds(at, part)],
                    load_sem.at[3 + 2 * chunk + side],
                )
            )
    scalar_load = pltpu.make_async_copy(order_hbm, order_scalar, load_sem.at[3 + 2 * CHUNKS])
    projection_load = pltpu.make_async_copy(projection_hbm, projection, load_sem.at[1])
    transfer_load = pltpu.make_async_copy(transfer_hbm, transfer, load_sem.at[2])
    for load in loads:
        load.start()
    scalar_load.start()
    projection_load.start()
    transfer_load.start()

    partners, bits = [], []
    for level in range(levels):
        span = 1 << level
        bit = lax.rem(lax.div(leaf, span), 2)
        bits.append(bit)
        partners.append(leaf + span - 2 * span * bit)
    peers = [lax.rem(panel + step, panels) for step in range(1, panels)]
    own_at = [pl.ds(pl.multiple_of(bit * rank, rank), rank) for bit in bits]
    other_at = [pl.ds(pl.multiple_of((1 - bit) * rank, rank), rank) for bit in bits]

    barrier = pltpu.get_barrier_semaphore()
    for partner in partners:
        pl.semaphore_signal(barrier, inc=1, device_id=(panel, partner), device_id_type=MESH)
    for peer in peers:
        pl.semaphore_signal(barrier, inc=1, device_id=(peer, leaf), device_id_type=MESH)

    loads[0].wait()
    for start in range(0, rows, 128):
        row = order[:, start:start + 128]
        order_wide[start:start + 128, :] = jnp.broadcast_to(row, (128, 128)).T.astype(jnp.int16)
    for load in loads[1:]:
        load.wait()

    pl.semaphore_wait(barrier, levels + panels - 1)
    matrix_copy = pltpu.make_async_remote_copy(
        src_ref=transfer_hbm.at[top, :, :, other_at[top]],
        dst_ref=crossing,
        send_sem=matrix_sem.at[0],
        recv_sem=matrix_sem.at[1],
        device_id=(panel, partners[top]),
        device_id_type=MESH,
    )
    matrix_copy.start()

    source_tile = tile_of(rows, 512)
    for start in range(0, rows, source_tile):
        turned = excitation[:, start:start + source_tile].T
        points[start:start + source_tile, :] = turned
        points_wide[start:start + source_tile, :] = turned.astype(jnp.float32)
    scalar_load.wait()

    tile = tile_of(rows, 512)
    read = picked.shape[0]

    def gather(step, carry):
        begin = pl.multiple_of(step * tile, tile)
        for base in range(0, read, GROUP):
            found = [
                points_wide[pl.ds(order_scalar[0, begin + base + row], 1), :] for row in range(GROUP)
            ]
            for row in range(GROUP):
                picked[base + row:base + row + 1, :] = found[row]
        wanted = order_wide[pl.ds(begin + read, tile - read), :]
        lane = lax.broadcasted_iota(jnp.int32, wanted.shape, 1).astype(jnp.int16)
        one = jnp.ones(wanted.shape, jnp.bfloat16)
        zero = jnp.zeros(wanted.shape, jnp.bfloat16)
        chosen = jnp.concatenate(
            [jnp.where(wanted == lane + jnp.int16(start), one, zero) for start in range(0, rows, 128)], axis=1
        )
        ordered[pl.ds(begin + read, tile - read), :] = jnp.dot(
            chosen, points[...], preferred_element_type=jnp.float32
        ).astype(jnp.bfloat16)
        ordered[pl.ds(begin, read), :] = picked[...].astype(jnp.bfloat16)
        return carry

    lax.fori_loop(0, rows // tile, gather, 0)

    projection_load.wait()
    level_zero = jnp.dot(
        projection[...].reshape(2 * rank, rows), ordered[...], preferred_element_type=jnp.float32
    )

    def level_copy(level, chunk):
        return pltpu.make_async_remote_copy(
            src_ref=held.at[level, chunk],
            dst_ref=arrived.at[level, chunk],
            send_sem=level_send.at[level, chunk],
            recv_sem=level_recv.at[level, chunk],
            device_id=(panel, partners[level]),
            device_id_type=MESH,
        )

    piece = rank // panels

    def scatter_copy(step, chunk):
        return pltpu.make_async_remote_copy(
            src_ref=partial.at[chunk, :, pl.ds(pl.multiple_of(peers[step] * piece, piece), piece)],
            dst_ref=scattered.at[step, chunk],
            send_sem=scatter_send.at[step, chunk],
            recv_sem=scatter_recv.at[step, chunk],
            device_id=(peers[step], leaf),
            device_id_type=MESH,
        )

    def cross_copy(chunk):
        return pltpu.make_async_remote_copy(
            src_ref=cross_out.at[chunk],
            dst_ref=cross_in.at[chunk],
            send_sem=cross_send.at[chunk],
            recv_sem=cross_recv.at[chunk],
            device_id=(panel, partners[top]),
            device_id_type=MESH,
        )

    mine = pl.ds(pl.multiple_of(panel * piece, piece), piece)

    def gather_copy(step, chunk):
        return pltpu.make_async_remote_copy(
            src_ref=total.at[chunk, mine],
            dst_ref=total.at[chunk, mine],
            send_sem=gather_send.at[step, chunk],
            recv_sem=gather_recv.at[step, chunk],
            device_id=(peers[step], leaf),
            device_id_type=MESH,
        )

    def product(matrix, block):
        return jnp.dot(matrix.reshape(2 * rank, rank), block, preferred_element_type=jnp.float32)

    for chunk in range(CHUNKS):
        held[0, chunk] = combine(level_zero[:, chunk * wide:(chunk + 1) * wide], rank, part)
        if top > 0:
            level_copy(0, chunk).start()
    transfer_load.wait()
    for level in range(top):
        own = [product(transfer[level, :, :, own_at[level]], held[level, chunk]) for chunk in range(CHUNKS)]
        for chunk in range(CHUNKS):
            level_copy(level, chunk).wait_recv()
            other = product(transfer[level, :, :, other_at[level]], arrived[level, chunk])
            held[level + 1, chunk] = combine(own[chunk] + other, rank, part)
            if level + 1 < top:
                level_copy(level + 1, chunk).start()
            else:
                if chunk == 0:
                    matrix_copy.wait_recv()
                partial[chunk, 0] = combine(
                    product(transfer[top, :, :, own_at[top]], held[top, chunk]), rank, part
                )
                partial[chunk, 1] = combine(product(crossing[...], held[top, chunk]), rank, part)
                for step in range(panels - 1):
                    scatter_copy(step, chunk).start()
    kept = []
    for chunk in range(CHUNKS):
        sums = [partial[chunk, side, mine].astype(jnp.float32) for side in range(2)]
        for step in range(panels - 1):
            scatter_copy(step, chunk).wait_recv()
            sums = [sums[side] + scattered[step, chunk, side].astype(jnp.float32) for side in range(2)]
        cross_out[chunk] = sums[1].astype(jnp.bfloat16)
        cross_copy(chunk).start()
        kept.append(sums[0])
    for chunk in range(CHUNKS):
        cross_copy(chunk).wait_recv()
        total[chunk, mine] = (kept[chunk] + cross_in[chunk].astype(jnp.float32)).astype(jnp.bfloat16)
        for step in range(panels - 1):
            gather_copy(step, chunk).start()
    for chunk in range(CHUNKS):
        for step in range(panels - 1):
            gather_copy(step, chunk).wait_recv()
        turned = total[chunk].T
        for side in range(2):
            at = side * exc + chunk * part
            out_ref[at:at + part, :] = turned[side * part:(side + 1) * part]
    matrix_copy.wait_send()
    for chunk in range(CHUNKS):
        for level in range(top):
            level_copy(level, chunk).wait_send()
        cross_copy(chunk).wait_send()
        for step in range(panels - 1):
            scatter_copy(step, chunk).wait_send()
            gather_copy(step, chunk).wait_send()


def expansion_kernel(total_hbm, expansion_ref, out_hbm, total_ref, out, load_sem, store_sem):
    load = pltpu.make_async_copy(total_hbm, total_ref, load_sem)
    load.start()
    load.wait()
    exc = total_ref.shape[0] // 2
    rows = expansion_ref.shape[2]
    columns = tile_of(rows, 768)
    stores = []
    for step in range(rows // columns):
        span = slice(step * columns, (step + 1) * columns)
        first = jnp.dot(total_ref[...], expansion_ref[0, :, span], preferred_element_type=jnp.float32)
        second = jnp.dot(total_ref[...], expansion_ref[1, :, span], preferred_element_type=jnp.float32)
        out[0, :, span] = (first[:exc] - second[exc:]).astype(out.dtype)
        out[1, :, span] = (second[:exc] + first[exc:]).astype(out.dtype)
        at = pl.ds(step * columns, columns)
        store = pltpu.make_async_copy(out.at[:, :, at], out_hbm.at[:, :, at], store_sem.at[step])
        store.start()
        stores.append(store)
    for store in stores:
        store.wait()


def per_device(excitation, point_order, projection, transfer, expansion):
    panels = lax.axis_size("panel")
    levels = transfer.shape[0]
    _, exc, rows = excitation.shape
    rank = projection.shape[1]
    wide = 2 * exc // CHUNKS
    piece = rank // panels
    total = pl.pallas_call(
        functools.partial(coefficients_kernel, panels, levels),
        out_shape=jax.ShapeDtypeStruct((2 * exc, rank), jnp.bfloat16),
        in_specs=[pl.BlockSpec(memory_space=pl.ANY)] * 4,
        out_specs=pl.BlockSpec(memory_space=pltpu.VMEM),
        scratch_shapes=[
            pltpu.VMEM((2 * exc, rows), jnp.bfloat16),
            pltpu.VMEM((1, rows), jnp.int32),
            pltpu.SMEM((1, rows), jnp.int32),
            pltpu.VMEM(projection.shape, jnp.bfloat16),
            pltpu.VMEM(transfer.shape, jnp.bfloat16),
            pltpu.VMEM((2, rank, rank), jnp.bfloat16),
            pltpu.VMEM((rows, 2 * exc), jnp.bfloat16),
            pltpu.VMEM((rows, 2 * exc), jnp.float32),
            pltpu.VMEM((tile_of(rows, 512) // 2, 2 * exc), jnp.float32),
            pltpu.VMEM((rows, 128), jnp.int16),
            pltpu.VMEM((rows, 2 * exc), jnp.bfloat16),
            pltpu.VMEM((levels, CHUNKS, rank, wide), jnp.bfloat16),
            pltpu.VMEM((levels, CHUNKS, rank, wide), jnp.bfloat16),
            pltpu.VMEM((CHUNKS, 2, rank, wide), jnp.bfloat16),
            pltpu.VMEM((panels - 1, CHUNKS, 2, piece, wide), jnp.bfloat16),
            pltpu.VMEM((CHUNKS, piece, wide), jnp.bfloat16),
            pltpu.VMEM((CHUNKS, piece, wide), jnp.bfloat16),
            pltpu.VMEM((CHUNKS, rank, wide), jnp.bfloat16),
            pltpu.SemaphoreType.DMA((4 + 2 * CHUNKS,)),
            pltpu.SemaphoreType.DMA((2,)),
            pltpu.SemaphoreType.DMA((levels, CHUNKS)),
            pltpu.SemaphoreType.DMA((levels, CHUNKS)),
            pltpu.SemaphoreType.DMA((panels - 1, CHUNKS)),
            pltpu.SemaphoreType.DMA((panels - 1, CHUNKS)),
            pltpu.SemaphoreType.DMA((CHUNKS,)),
            pltpu.SemaphoreType.DMA((CHUNKS,)),
            pltpu.SemaphoreType.DMA((panels - 1, CHUNKS)),
            pltpu.SemaphoreType.DMA((panels - 1, CHUNKS)),
        ],
        compiler_params=pltpu.CompilerParams(
            collective_id=0, has_side_effects=True, vmem_limit_bytes=60 * MIB
        ),
    )(excitation, point_order, projection, transfer)
    return pl.pallas_call(
        expansion_kernel,
        out_shape=jax.ShapeDtypeStruct((2, exc, rows), jnp.bfloat16),
        in_specs=[pl.BlockSpec(memory_space=pl.ANY), pl.BlockSpec(memory_space=pltpu.VMEM)],
        out_specs=pl.BlockSpec(memory_space=pl.ANY),
        scratch_shapes=[
            pltpu.VMEM((2 * exc, rank), jnp.bfloat16),
            pltpu.VMEM((2, exc, rows), jnp.bfloat16),
            pltpu.SemaphoreType.DMA,
            pltpu.SemaphoreType.DMA((rows // tile_of(rows, 768),)),
        ],
        compiler_params=pltpu.CompilerParams(vmem_limit_bytes=24 * MIB),
    )(total, expansion)


def solution(mesh):
    in_specs = (
        P(None, None, ("panel", "leaf")),
        P(("panel", "leaf"), None),
        P(None, None, ("panel", "leaf")),
        P(None, None, ("panel", "leaf"), None),
        P(None, None, ("panel", "leaf")),
    )
    out_specs = P(None, None, ("panel", "leaf"))
    return jax.shard_map(
        per_device, mesh=mesh, in_specs=in_specs, out_specs=out_specs, check_vma=False
    )
```

```python
import functools

import jax
import jax.numpy as jnp
from jax import lax
from jax.experimental import pallas as pl
from jax.experimental.pallas import tpu as pltpu
from jax.sharding import PartitionSpec as P

MESH = pl.DeviceIdType.MESH
CHUNKS = 2
GROUP = 16
MIB = 1 << 20


def tile_of(extent, most, unit=128):
    tile = most
    while extent % tile or tile % unit:
        tile -= unit
    return tile


def combine(product, rank, width):
    real = product[:rank, :width] - product[rank:, width:]
    imag = product[:rank, width:] + product[rank:, :width]
    return jnp.concatenate((real, imag), axis=1).astype(jnp.bfloat16)


def coefficients_kernel(
    panels, levels,
    excitation_hbm, order_hbm, projection_hbm, transfer_hbm, out_ref,
    excitation, order, order_scalar, projection, transfer, points, points_wide, picked, order_wide, ordered,
    held, arrived, scattered, total,
    load_sem, level_send, level_recv, scatter_send, scatter_recv,
    gather_send, gather_recv,
):
    panel = lax.axis_index("panel")
    leaf = lax.axis_index("leaf")
    _, exc, rows = excitation_hbm.shape
    rank = projection.shape[1]
    part = exc // CHUNKS
    wide = 2 * part

    loads = [pltpu.make_async_copy(order_hbm, order, load_sem.at[0])]
    for chunk in range(CHUNKS):
        for side in range(2):
            at = chunk * wide + side * part
            loads.append(
                pltpu.make_async_copy(
                    excitation_hbm.at[side, pl.ds(chunk * part, part)], excitation.at[pl.ds(at, part)],
                    load_sem.at[3 + 2 * chunk + side],
                )
            )
    scalar_load = pltpu.make_async_copy(order_hbm, order_scalar, load_sem.at[3 + 2 * CHUNKS])
    projection_load = pltpu.make_async_copy(projection_hbm, projection, load_sem.at[1])
    transfer_load = pltpu.make_async_copy(transfer_hbm, transfer, load_sem.at[2])
    for load in loads:
        load.start()
    scalar_load.start()
    projection_load.start()
    transfer_load.start()

    partners, bits = [], []
    for level in range(levels):
        span = 1 << level
        bit = lax.rem(lax.div(leaf, span), 2)
        bits.append(bit)
        partners.append(leaf + span - 2 * span * bit)
    peers = [lax.rem(panel + step, panels) for step in range(1, panels)]
    own_at = [pl.ds(pl.multiple_of(bit * rank, rank), rank) for bit in bits]
    other_at = [pl.ds(pl.multiple_of((1 - bit) * rank, rank), rank) for bit in bits]

    barrier = pltpu.get_barrier_semaphore()
    for partner in partners:
        pl.semaphore_signal(barrier, inc=1, device_id=(panel, partner), device_id_type=MESH)
    for peer in peers:
        pl.semaphore_signal(barrier, inc=1, device_id=(peer, leaf), device_id_type=MESH)

    loads[0].wait()
    for start in range(0, rows, 128):
        row = order[:, start:start + 128]
        order_wide[start:start + 128, :] = jnp.broadcast_to(row, (128, 128)).T.astype(jnp.int16)
    for load in loads[1:]:
        load.wait()

    source_tile = tile_of(rows, 512)
    for start in range(0, rows, source_tile):
        turned = excitation[:, start:start + source_tile].T
        points[start:start + source_tile, :] = turned
        points_wide[start:start + source_tile, :] = turned.astype(jnp.float32)
    scalar_load.wait()

    tile = tile_of(rows, 512)
    read = picked.shape[0]

    def gather(step, carry):
        begin = pl.multiple_of(step * tile, tile)
        for base in range(0, read, GROUP):
            found = [
                points_wide[pl.ds(order_scalar[0, begin + base + row], 1), :] for row in range(GROUP)
            ]
            for row in range(GROUP):
                picked[base + row:base + row + 1, :] = found[row]
        wanted = order_wide[pl.ds(begin + read, tile - read), :]
        lane = lax.broadcasted_iota(jnp.int32, wanted.shape, 1).astype(jnp.int16)
        one = jnp.ones(wanted.shape, jnp.bfloat16)
        zero = jnp.zeros(wanted.shape, jnp.bfloat16)
        chosen = jnp.concatenate(
            [jnp.where(wanted == lane + jnp.int16(start), one, zero) for start in range(0, rows, 128)], axis=1
        )
        ordered[pl.ds(begin + read, tile - read), :] = jnp.dot(
            chosen, points[...], preferred_element_type=jnp.float32
        ).astype(jnp.bfloat16)
        ordered[pl.ds(begin, read), :] = picked[...].astype(jnp.bfloat16)
        return carry

    lax.fori_loop(0, rows // tile, gather, 0)

    projection_load.wait()
    level_zero = jnp.dot(
        projection[...].reshape(2 * rank, rows), ordered[...], preferred_element_type=jnp.float32
    )

    def level_copy(level, chunk):
        return pltpu.make_async_remote_copy(
            src_ref=held.at[level, chunk],
            dst_ref=arrived.at[level, chunk],
            send_sem=level_send.at[level, chunk],
            recv_sem=level_recv.at[level, chunk],
            device_id=(panel, partners[level]),
            device_id_type=MESH,
        )

    piece = rank // panels

    def scatter_copy(step, chunk):
        return pltpu.make_async_remote_copy(
            src_ref=held.at[levels, chunk, pl.ds(pl.multiple_of(peers[step] * piece, piece), piece)],
            dst_ref=scattered.at[step, chunk],
            send_sem=scatter_send.at[step, chunk],
            recv_sem=scatter_recv.at[step, chunk],
            device_id=(peers[step], leaf),
            device_id_type=MESH,
        )

    mine = pl.ds(pl.multiple_of(panel * piece, piece), piece)

    def gather_copy(step, chunk):
        return pltpu.make_async_remote_copy(
            src_ref=total.at[chunk, mine],
            dst_ref=total.at[chunk, mine],
            send_sem=gather_send.at[step, chunk],
            recv_sem=gather_recv.at[step, chunk],
            device_id=(peers[step], leaf),
            device_id_type=MESH,
        )

    def product(matrix, block):
        return jnp.dot(matrix.reshape(2 * rank, rank), block, preferred_element_type=jnp.float32)

    pl.semaphore_wait(barrier, levels + panels - 1)

    def send_on(level, chunk):
        if level < levels:
            level_copy(level, chunk).start()
        else:
            for step in range(panels - 1):
                scatter_copy(step, chunk).start()

    for chunk in range(CHUNKS):
        held[0, chunk] = combine(level_zero[:, chunk * wide:(chunk + 1) * wide], rank, part)
        send_on(0, chunk)
    transfer_load.wait()
    for level in range(levels):
        own = [product(transfer[level, :, :, own_at[level]], held[level, chunk]) for chunk in range(CHUNKS)]
        for chunk in range(CHUNKS):
            level_copy(level, chunk).wait_recv()
            other = product(transfer[level, :, :, other_at[level]], arrived[level, chunk])
            held[level + 1, chunk] = combine(own[chunk] + other, rank, part)
            send_on(level + 1, chunk)
    for chunk in range(CHUNKS):
        summed = held[levels, chunk, mine].astype(jnp.float32)
        for step in range(panels - 1):
            scatter_copy(step, chunk).wait_recv()
            summed = summed + scattered[step, chunk].astype(jnp.float32)
        total[chunk, mine] = summed.astype(jnp.bfloat16)
        for step in range(panels - 1):
            gather_copy(step, chunk).start()
    for chunk in range(CHUNKS):
        for step in range(panels - 1):
            gather_copy(step, chunk).wait_recv()
        turned = total[chunk].T
        for side in range(2):
            at = side * exc + chunk * part
            out_ref[at:at + part, :] = turned[side * part:(side + 1) * part]
    for chunk in range(CHUNKS):
        for level in range(levels):
            level_copy(level, chunk).wait_send()
        for step in range(panels - 1):
            scatter_copy(step, chunk).wait_send()
            gather_copy(step, chunk).wait_send()


def expansion_kernel(total_hbm, expansion_ref, out_hbm, total_ref, out, load_sem, store_sem):
    load = pltpu.make_async_copy(total_hbm, total_ref, load_sem)
    load.start()
    load.wait()
    exc = total_ref.shape[0] // 2
    rows = expansion_ref.shape[2]
    columns = tile_of(rows, 768)
    stores = []
    for step in range(rows // columns):
        span = slice(step * columns, (step + 1) * columns)
        first = jnp.dot(total_ref[...], expansion_ref[0, :, span], preferred_element_type=jnp.float32)
        second = jnp.dot(total_ref[...], expansion_ref[1, :, span], preferred_element_type=jnp.float32)
        out[0, :, span] = (first[:exc] - second[exc:]).astype(out.dtype)
        out[1, :, span] = (second[:exc] + first[exc:]).astype(out.dtype)
        at = pl.ds(step * columns, columns)
        store = pltpu.make_async_copy(out.at[:, :, at], out_hbm.at[:, :, at], store_sem.at[step])
        store.start()
        stores.append(store)
    for store in stores:
        store.wait()


def per_device(excitation, point_order, projection, transfer, expansion):
    panels = lax.axis_size("panel")
    levels = transfer.shape[0]
    _, exc, rows = excitation.shape
    rank = projection.shape[1]
    wide = 2 * exc // CHUNKS
    piece = rank // panels
    total = pl.pallas_call(
        functools.partial(coefficients_kernel, panels, levels),
        out_shape=jax.ShapeDtypeStruct((2 * exc, rank), jnp.bfloat16),
        in_specs=[pl.BlockSpec(memory_space=pl.ANY)] * 4,
        out_specs=pl.BlockSpec(memory_space=pltpu.VMEM),
        scratch_shapes=[
            pltpu.VMEM((2 * exc, rows), jnp.bfloat16),
            pltpu.VMEM((1, rows), jnp.int32),
            pltpu.SMEM((1, rows), jnp.int32),
            pltpu.VMEM(projection.shape, jnp.bfloat16),
            pltpu.VMEM(transfer.shape, jnp.bfloat16),
            pltpu.VMEM((rows, 2 * exc), jnp.bfloat16),
            pltpu.VMEM((rows, 2 * exc), jnp.float32),
            pltpu.VMEM((tile_of(rows, 512) // 2, 2 * exc), jnp.float32),
            pltpu.VMEM((rows, 128), jnp.int16),
            pltpu.VMEM((rows, 2 * exc), jnp.bfloat16),
            pltpu.VMEM((levels + 1, CHUNKS, rank, wide), jnp.bfloat16),
            pltpu.VMEM((levels, CHUNKS, rank, wide), jnp.bfloat16),
            pltpu.VMEM((panels - 1, CHUNKS, piece, wide), jnp.bfloat16),
            pltpu.VMEM((CHUNKS, rank, wide), jnp.bfloat16),
            pltpu.SemaphoreType.DMA((4 + 2 * CHUNKS,)),
            pltpu.SemaphoreType.DMA((levels, CHUNKS)),
            pltpu.SemaphoreType.DMA((levels, CHUNKS)),
            pltpu.SemaphoreType.DMA((panels - 1, CHUNKS)),
            pltpu.SemaphoreType.DMA((panels - 1, CHUNKS)),
            pltpu.SemaphoreType.DMA((panels - 1, CHUNKS)),
            pltpu.SemaphoreType.DMA((panels - 1, CHUNKS)),
        ],
        compiler_params=pltpu.CompilerParams(
            collective_id=0, has_side_effects=True, vmem_limit_bytes=60 * MIB
        ),
    )(excitation, point_order, projection, transfer)
    return pl.pallas_call(
        expansion_kernel,
        out_shape=jax.ShapeDtypeStruct((2, exc, rows), jnp.bfloat16),
        in_specs=[pl.BlockSpec(memory_space=pl.ANY), pl.BlockSpec(memory_space=pltpu.VMEM)],
        out_specs=pl.BlockSpec(memory_space=pl.ANY),
        scratch_shapes=[
            pltpu.VMEM((2 * exc, rank), jnp.bfloat16),
            pltpu.VMEM((2, exc, rows), jnp.bfloat16),
            pltpu.SemaphoreType.DMA,
            pltpu.SemaphoreType.DMA((rows // tile_of(rows, 768),)),
        ],
        compiler_params=pltpu.CompilerParams(vmem_limit_bytes=24 * MIB),
    )(total, expansion)


def solution(mesh):
    in_specs = (
        P(None, None, ("panel", "leaf")),
        P(("panel", "leaf"), None),
        P(None, None, ("panel", "leaf")),
        P(None, None, ("panel", "leaf"), None),
        P(None, None, ("panel", "leaf")),
    )
    out_specs = P(None, None, ("panel", "leaf"))
    return jax.shard_map(
        per_device, mesh=mesh, in_specs=in_specs, out_specs=out_specs, check_vma=False
    )
```

```python
import functools

import jax
import jax.numpy as jnp
from jax import lax
from jax.experimental import pallas as pl
from jax.experimental.pallas import tpu as pltpu
from jax.sharding import PartitionSpec as P

MESH = pl.DeviceIdType.MESH
CHUNKS = 2
MIB = 1 << 20


def tile_of(extent, most, unit=128):
    tile = most
    while extent % tile or tile % unit:
        tile -= unit
    return tile


def combine(product, rank, width):
    real = product[:rank, :width] - product[rank:, width:]
    imag = product[:rank, width:] + product[rank:, :width]
    return jnp.concatenate((real, imag), axis=1).astype(jnp.bfloat16)


def coefficients_kernel(
    panels, levels,
    excitation_hbm, order_hbm, projection_hbm, transfer_hbm, out_ref,
    excitation, order, projection, transfer, crossing, points, order_wide, ordered,
    held, arrived, partial, scattered, cross_out, cross_in, total,
    load_sem, matrix_sem, level_send, level_recv, scatter_send, scatter_recv,
    cross_send, cross_recv, gather_send, gather_recv,
):
    panel = lax.axis_index("panel")
    leaf = lax.axis_index("leaf")
    _, exc, rows = excitation_hbm.shape
    rank = projection.shape[1]
    part = exc // CHUNKS
    wide = 2 * part
    top = levels - 1

    loads = [pltpu.make_async_copy(order_hbm, order, load_sem.at[0])]
    for chunk in range(CHUNKS):
        for side in range(2):
            at = chunk * wide + side * part
            loads.append(
                pltpu.make_async_copy(
                    excitation_hbm.at[side, pl.ds(chunk * part, part)], excitation.at[pl.ds(at, part)],
                    load_sem.at[3 + 2 * chunk + side],
                )
            )
    projection_load = pltpu.make_async_copy(projection_hbm, projection, load_sem.at[1])
    transfer_load = pltpu.make_async_copy(transfer_hbm, transfer, load_sem.at[2])
    for load in loads:
        load.start()
    projection_load.start()
    transfer_load.start()

    partners, bits = [], []
    for level in range(levels):
        span = 1 << level
        bit = lax.rem(lax.div(leaf, span), 2)
        bits.append(bit)
        partners.append(leaf + span - 2 * span * bit)
    peers = [lax.rem(panel + step, panels) for step in range(1, panels)]
    own_at = [pl.ds(pl.multiple_of(bit * rank, rank), rank) for bit in bits]
    other_at = [pl.ds(pl.multiple_of((1 - bit) * rank, rank), rank) for bit in bits]

    barrier = pltpu.get_barrier_semaphore()
    for partner in partners:
        pl.semaphore_signal(barrier, inc=1, device_id=(panel, partner), device_id_type=MESH)
    for peer in peers:
        pl.semaphore_signal(barrier, inc=1, device_id=(peer, leaf), device_id_type=MESH)

    loads[0].wait()
    for start in range(0, rows, 128):
        row = order[:, start:start + 128]
        order_wide[start:start + 128, :] = jnp.broadcast_to(row, (128, 128)).T.astype(jnp.int16)
    for load in loads[1:]:
        load.wait()

    pl.semaphore_wait(barrier, levels + panels - 1)
    matrix_copy = pltpu.make_async_remote_copy(
        src_ref=transfer_hbm.at[top, :, :, other_at[top]],
        dst_ref=crossing,
        send_sem=matrix_sem.at[0],
        recv_sem=matrix_sem.at[1],
        device_id=(panel, partners[top]),
        device_id_type=MESH,
    )
    matrix_copy.start()

    source_tile = tile_of(rows, 512)
    for start in range(0, rows, source_tile):
        points[start:start + source_tile, :] = excitation[:, start:start + source_tile].T

    tile = tile_of(rows, 512)
    lane = lax.broadcasted_iota(jnp.int32, (tile, 128), 1).astype(jnp.int16)
    one = jnp.ones((tile, 128), jnp.bfloat16)
    zero = jnp.zeros((tile, 128), jnp.bfloat16)
    for begin in range(0, rows, tile):
        wanted = order_wide[begin:begin + tile, :]
        chosen = jnp.concatenate(
            [jnp.where(wanted == lane + jnp.int16(start), one, zero) for start in range(0, rows, 128)], axis=1
        )
        ordered[begin:begin + tile, :] = jnp.dot(
            chosen, points[...], preferred_element_type=jnp.float32
        ).astype(jnp.bfloat16)

    projection_load.wait()
    level_zero = jnp.dot(
        projection[...].reshape(2 * rank, rows), ordered[...], preferred_element_type=jnp.float32
    )

    def level_copy(level, chunk):
        return pltpu.make_async_remote_copy(
            src_ref=held.at[level, chunk],
            dst_ref=arrived.at[level, chunk],
            send_sem=level_send.at[level, chunk],
            recv_sem=level_recv.at[level, chunk],
            device_id=(panel, partners[level]),
            device_id_type=MESH,
        )

    piece = rank // panels

    def scatter_copy(step, chunk):
        return pltpu.make_async_remote_copy(
            src_ref=partial.at[chunk, :, pl.ds(pl.multiple_of(peers[step] * piece, piece), piece)],
            dst_ref=scattered.at[step, chunk],
            send_sem=scatter_send.at[step, chunk],
            recv_sem=scatter_recv.at[step, chunk],
            device_id=(peers[step], leaf),
            device_id_type=MESH,
        )

    def cross_copy(chunk):
        return pltpu.make_async_remote_copy(
            src_ref=cross_out.at[chunk],
            dst_ref=cross_in.at[chunk],
            send_sem=cross_send.at[chunk],
            recv_sem=cross_recv.at[chunk],
            device_id=(panel, partners[top]),
            device_id_type=MESH,
        )

    mine = pl.ds(pl.multiple_of(panel * piece, piece), piece)

    def gather_copy(step, chunk):
        return pltpu.make_async_remote_copy(
            src_ref=total.at[chunk, mine],
            dst_ref=total.at[chunk, mine],
            send_sem=gather_send.at[step, chunk],
            recv_sem=gather_recv.at[step, chunk],
            device_id=(peers[step], leaf),
            device_id_type=MESH,
        )

    def product(matrix, block):
        return jnp.dot(matrix.reshape(2 * rank, rank), block, preferred_element_type=jnp.float32)

    for chunk in range(CHUNKS):
        held[0, chunk] = combine(level_zero[:, chunk * wide:(chunk + 1) * wide], rank, part)
        if top > 0:
            level_copy(0, chunk).start()
    transfer_load.wait()
    for level in range(top):
        own = [product(transfer[level, :, :, own_at[level]], held[level, chunk]) for chunk in range(CHUNKS)]
        for chunk in range(CHUNKS):
            level_copy(level, chunk).wait_recv()
            other = product(transfer[level, :, :, other_at[level]], arrived[level, chunk])
            held[level + 1, chunk] = combine(own[chunk] + other, rank, part)
            if level + 1 < top:
                level_copy(level + 1, chunk).start()
            else:
                if chunk == 0:
                    matrix_copy.wait_recv()
                partial[chunk, 0] = combine(
                    product(transfer[top, :, :, own_at[top]], held[top, chunk]), rank, part
                )
                partial[chunk, 1] = combine(product(crossing[...], held[top, chunk]), rank, part)
                for step in range(panels - 1):
                    scatter_copy(step, chunk).start()
    kept = []
    for chunk in range(CHUNKS):
        sums = [partial[chunk, side, mine].astype(jnp.float32) for side in range(2)]
        for step in range(panels - 1):
            scatter_copy(step, chunk).wait_recv()
            sums = [sums[side] + scattered[step, chunk, side].astype(jnp.float32) for side in range(2)]
        cross_out[chunk] = sums[1].astype(jnp.bfloat16)
        cross_copy(chunk).start()
        kept.append(sums[0])
    for chunk in range(CHUNKS):
        cross_copy(chunk).wait_recv()
        total[chunk, mine] = (kept[chunk] + cross_in[chunk].astype(jnp.float32)).astype(jnp.bfloat16)
        for step in range(panels - 1):
            gather_copy(step, chunk).start()
    for chunk in range(CHUNKS):
        for step in range(panels - 1):
            gather_copy(step, chunk).wait_recv()
        turned = total[chunk].T
        for side in range(2):
            at = side * exc + chunk * part
            out_ref[at:at + part, :] = turned[side * part:(side + 1) * part]
    matrix_copy.wait_send()
    for chunk in range(CHUNKS):
        for level in range(top):
            level_copy(level, chunk).wait_send()
        cross_copy(chunk).wait_send()
        for step in range(panels - 1):
            scatter_copy(step, chunk).wait_send()
            gather_copy(step, chunk).wait_send()


def expansion_kernel(total_hbm, expansion_ref, out_hbm, total_ref, out, load_sem, store_sem):
    load = pltpu.make_async_copy(total_hbm, total_ref, load_sem)
    load.start()
    load.wait()
    exc = total_ref.shape[0] // 2
    rows = expansion_ref.shape[2]
    columns = tile_of(rows, 768)
    stores = []
    for step in range(rows // columns):
        span = slice(step * columns, (step + 1) * columns)
        first = jnp.dot(total_ref[...], expansion_ref[0, :, span], preferred_element_type=jnp.float32)
        second = jnp.dot(total_ref[...], expansion_ref[1, :, span], preferred_element_type=jnp.float32)
        out[0, :, span] = (first[:exc] - second[exc:]).astype(out.dtype)
        out[1, :, span] = (second[:exc] + first[exc:]).astype(out.dtype)
        at = pl.ds(step * columns, columns)
        store = pltpu.make_async_copy(out.at[:, :, at], out_hbm.at[:, :, at], store_sem.at[step])
        store.start()
        stores.append(store)
    for store in stores:
        store.wait()


def per_device(excitation, point_order, projection, transfer, expansion):
    panels = lax.axis_size("panel")
    levels = transfer.shape[0]
    _, exc, rows = excitation.shape
    rank = projection.shape[1]
    wide = 2 * exc // CHUNKS
    piece = rank // panels
    total = pl.pallas_call(
        functools.partial(coefficients_kernel, panels, levels),
        out_shape=jax.ShapeDtypeStruct((2 * exc, rank), jnp.bfloat16),
        in_specs=[pl.BlockSpec(memory_space=pl.ANY)] * 4,
        out_specs=pl.BlockSpec(memory_space=pltpu.VMEM),
        scratch_shapes=[
            pltpu.VMEM((2 * exc, rows), jnp.bfloat16),
            pltpu.VMEM((1, rows), jnp.int32),
            pltpu.VMEM(projection.shape, jnp.bfloat16),
            pltpu.VMEM(transfer.shape, jnp.bfloat16),
            pltpu.VMEM((2, rank, rank), jnp.bfloat16),
            pltpu.VMEM((rows, 2 * exc), jnp.bfloat16),
            pltpu.VMEM((rows, 128), jnp.int16),
            pltpu.VMEM((rows, 2 * exc), jnp.bfloat16),
            pltpu.VMEM((levels, CHUNKS, rank, wide), jnp.bfloat16),
            pltpu.VMEM((levels, CHUNKS, rank, wide), jnp.bfloat16),
            pltpu.VMEM((CHUNKS, 2, rank, wide), jnp.bfloat16),
            pltpu.VMEM((panels - 1, CHUNKS, 2, piece, wide), jnp.bfloat16),
            pltpu.VMEM((CHUNKS, piece, wide), jnp.bfloat16),
            pltpu.VMEM((CHUNKS, piece, wide), jnp.bfloat16),
            pltpu.VMEM((CHUNKS, rank, wide), jnp.bfloat16),
            pltpu.SemaphoreType.DMA((3 + 2 * CHUNKS,)),
            pltpu.SemaphoreType.DMA((2,)),
            pltpu.SemaphoreType.DMA((levels, CHUNKS)),
            pltpu.SemaphoreType.DMA((levels, CHUNKS)),
            pltpu.SemaphoreType.DMA((panels - 1, CHUNKS)),
            pltpu.SemaphoreType.DMA((panels - 1, CHUNKS)),
            pltpu.SemaphoreType.DMA((CHUNKS,)),
            pltpu.SemaphoreType.DMA((CHUNKS,)),
            pltpu.SemaphoreType.DMA((panels - 1, CHUNKS)),
            pltpu.SemaphoreType.DMA((panels - 1, CHUNKS)),
        ],
        compiler_params=pltpu.CompilerParams(
            collective_id=0, has_side_effects=True, vmem_limit_bytes=60 * MIB
        ),
    )(excitation, point_order, projection, transfer)
    return pl.pallas_call(
        expansion_kernel,
        out_shape=jax.ShapeDtypeStruct((2, exc, rows), jnp.bfloat16),
        in_specs=[pl.BlockSpec(memory_space=pl.ANY), pl.BlockSpec(memory_space=pltpu.VMEM)],
        out_specs=pl.BlockSpec(memory_space=pl.ANY),
        scratch_shapes=[
            pltpu.VMEM((2 * exc, rank), jnp.bfloat16),
            pltpu.VMEM((2, exc, rows), jnp.bfloat16),
            pltpu.SemaphoreType.DMA,
            pltpu.SemaphoreType.DMA((rows // tile_of(rows, 768),)),
        ],
        compiler_params=pltpu.CompilerParams(vmem_limit_bytes=24 * MIB),
    )(total, expansion)


def solution(mesh):
    in_specs = (
        P(None, None, ("panel", "leaf")),
        P(("panel", "leaf"), None),
        P(None, None, ("panel", "leaf")),
        P(None, None, ("panel", "leaf"), None),
        P(None, None, ("panel", "leaf")),
    )
    out_specs = P(None, None, ("panel", "leaf"))
    return jax.shard_map(
        per_device, mesh=mesh, in_specs=in_specs, out_specs=out_specs, check_vma=False
    )
```

```python
import functools

import jax
import jax.numpy as jnp
from jax import lax
from jax.experimental import pallas as pl
from jax.experimental.pallas import tpu as pltpu
from jax.sharding import PartitionSpec as P

MESH = pl.DeviceIdType.MESH
CHUNKS = 2
MIB = 1 << 20


def tile_of(extent, most, unit=128):
    tile = most
    while extent % tile or tile % unit:
        tile -= unit
    return tile


def combine(product, rank, width):
    real = product[:rank, :width] - product[rank:, width:]
    imag = product[:rank, width:] + product[rank:, :width]
    return jnp.concatenate((real, imag), axis=1).astype(jnp.bfloat16)


def coefficients_kernel(
    panels, levels,
    excitation_hbm, order_hbm, projection_hbm, transfer_hbm, out_ref,
    excitation, order, projection, transfer, crossing, points, order_wide, ordered,
    held, arrived, partial, scattered, cross_out, cross_in, total,
    load_sem, matrix_sem, level_send, level_recv, scatter_send, scatter_recv,
    cross_send, cross_recv, gather_send, gather_recv,
):
    panel = lax.axis_index("panel")
    leaf = lax.axis_index("leaf")
    _, exc, rows = excitation_hbm.shape
    rank = projection.shape[1]
    part = exc // CHUNKS
    wide = 2 * part
    top = levels - 1

    loads = [pltpu.make_async_copy(order_hbm, order, load_sem.at[0])]
    for chunk in range(CHUNKS):
        for side in range(2):
            at = chunk * wide + side * part
            loads.append(
                pltpu.make_async_copy(
                    excitation_hbm.at[side, pl.ds(chunk * part, part)], excitation.at[pl.ds(at, part)],
                    load_sem.at[3 + 2 * chunk + side],
                )
            )
    projection_load = pltpu.make_async_copy(projection_hbm, projection, load_sem.at[1])
    transfer_load = pltpu.make_async_copy(transfer_hbm, transfer, load_sem.at[2])
    for load in loads:
        load.start()
    projection_load.start()
    transfer_load.start()

    partners, bits = [], []
    for level in range(levels):
        span = 1 << level
        bit = lax.rem(lax.div(leaf, span), 2)
        bits.append(bit)
        partners.append(leaf + span - 2 * span * bit)
    peers = [lax.rem(panel + step, panels) for step in range(1, panels)]
    own_at = [pl.ds(pl.multiple_of(bit * rank, rank), rank) for bit in bits]
    other_at = [pl.ds(pl.multiple_of((1 - bit) * rank, rank), rank) for bit in bits]

    barrier = pltpu.get_barrier_semaphore()
    for partner in partners:
        pl.semaphore_signal(barrier, inc=1, device_id=(panel, partner), device_id_type=MESH)
    for peer in peers:
        pl.semaphore_signal(barrier, inc=1, device_id=(peer, leaf), device_id_type=MESH)

    loads[0].wait()
    for start in range(0, rows, 128):
        row = order[:, start:start + 128]
        order_wide[start:start + 128, :] = jnp.broadcast_to(row, (128, 128)).T.astype(jnp.int16)

    pl.semaphore_wait(barrier, levels + panels - 1)
    matrix_copy = pltpu.make_async_remote_copy(
        src_ref=transfer_hbm.at[top, :, :, other_at[top]],
        dst_ref=crossing,
        send_sem=matrix_sem.at[0],
        recv_sem=matrix_sem.at[1],
        device_id=(panel, partners[top]),
        device_id_type=MESH,
    )
    matrix_copy.start()

    for load in loads[1:]:
        load.wait()
    source_tile = tile_of(rows, 512)
    for start in range(0, rows, source_tile):
        points[start:start + source_tile, :] = excitation[:, start:start + source_tile].T

    tile = tile_of(rows, 512)
    lane = lax.broadcasted_iota(jnp.int32, (tile, 128), 1).astype(jnp.int16)
    one = jnp.ones((tile, 128), jnp.bfloat16)
    zero = jnp.zeros((tile, 128), jnp.bfloat16)
    for begin in range(0, rows, tile):
        wanted = order_wide[begin:begin + tile, :]
        chosen = jnp.concatenate(
            [jnp.where(wanted == lane + jnp.int16(start), one, zero) for start in range(0, rows, 128)], axis=1
        )
        ordered[begin:begin + tile, :] = jnp.dot(
            chosen, points[...], preferred_element_type=jnp.float32
        ).astype(jnp.bfloat16)

    projection_load.wait()
    level_zero = jnp.dot(
        projection[...].reshape(2 * rank, rows), ordered[...], preferred_element_type=jnp.float32
    )

    def level_copy(level, chunk):
        return pltpu.make_async_remote_copy(
            src_ref=held.at[level, chunk],
            dst_ref=arrived.at[level, chunk],
            send_sem=level_send.at[level, chunk],
            recv_sem=level_recv.at[level, chunk],
            device_id=(panel, partners[level]),
            device_id_type=MESH,
        )

    piece = rank // panels

    def scatter_copy(step, chunk):
        return pltpu.make_async_remote_copy(
            src_ref=partial.at[chunk, :, pl.ds(pl.multiple_of(peers[step] * piece, piece), piece)],
            dst_ref=scattered.at[step, chunk],
            send_sem=scatter_send.at[step, chunk],
            recv_sem=scatter_recv.at[step, chunk],
            device_id=(peers[step], leaf),
            device_id_type=MESH,
        )

    def cross_copy(chunk):
        return pltpu.make_async_remote_copy(
            src_ref=cross_out.at[chunk],
            dst_ref=cross_in.at[chunk],
            send_sem=cross_send.at[chunk],
            recv_sem=cross_recv.at[chunk],
            device_id=(panel, partners[top]),
            device_id_type=MESH,
        )

    mine = pl.ds(pl.multiple_of(panel * piece, piece), piece)

    def gather_copy(step, chunk):
        return pltpu.make_async_remote_copy(
            src_ref=total.at[chunk, mine],
            dst_ref=total.at[chunk, mine],
            send_sem=gather_send.at[step, chunk],
            recv_sem=gather_recv.at[step, chunk],
            device_id=(peers[step], leaf),
            device_id_type=MESH,
        )

    def product(matrix, block):
        return jnp.dot(matrix.reshape(2 * rank, rank), block, preferred_element_type=jnp.float32)

    for chunk in range(CHUNKS):
        held[0, chunk] = combine(level_zero[:, chunk * wide:(chunk + 1) * wide], rank, part)
        if top > 0:
            level_copy(0, chunk).start()
    transfer_load.wait()
    for level in range(top):
        own = [product(transfer[level, :, :, own_at[level]], held[level, chunk]) for chunk in range(CHUNKS)]
        for chunk in range(CHUNKS):
            level_copy(level, chunk).wait_recv()
            other = product(transfer[level, :, :, other_at[level]], arrived[level, chunk])
            held[level + 1, chunk] = combine(own[chunk] + other, rank, part)
            if level + 1 < top:
                level_copy(level + 1, chunk).start()
            else:
                if chunk == 0:
                    matrix_copy.wait_recv()
                partial[chunk, 0] = combine(
                    product(transfer[top, :, :, own_at[top]], held[top, chunk]), rank, part
                )
                partial[chunk, 1] = combine(product(crossing[...], held[top, chunk]), rank, part)
                for step in range(panels - 1):
                    scatter_copy(step, chunk).start()
    kept = []
    for chunk in range(CHUNKS):
        sums = [partial[chunk, side, mine].astype(jnp.float32) for side in range(2)]
        for step in range(panels - 1):
            scatter_copy(step, chunk).wait_recv()
            sums = [sums[side] + scattered[step, chunk, side].astype(jnp.float32) for side in range(2)]
        cross_out[chunk] = sums[1].astype(jnp.bfloat16)
        cross_copy(chunk).start()
        kept.append(sums[0])
    for chunk in range(CHUNKS):
        cross_copy(chunk).wait_recv()
        total[chunk, mine] = (kept[chunk] + cross_in[chunk].astype(jnp.float32)).astype(jnp.bfloat16)
        for step in range(panels - 1):
            gather_copy(step, chunk).start()
    for chunk in range(CHUNKS):
        for step in range(panels - 1):
            gather_copy(step, chunk).wait_recv()
        turned = total[chunk].T
        for side in range(2):
            at = side * exc + chunk * part
            out_ref[at:at + part, :] = turned[side * part:(side + 1) * part]
    matrix_copy.wait_send()
    for chunk in range(CHUNKS):
        for level in range(top):
            level_copy(level, chunk).wait_send()
        cross_copy(chunk).wait_send()
        for step in range(panels - 1):
            scatter_copy(step, chunk).wait_send()
            gather_copy(step, chunk).wait_send()


def expansion_kernel(total_hbm, expansion_ref, out_hbm, total_ref, out, load_sem, store_sem):
    load = pltpu.make_async_copy(total_hbm, total_ref, load_sem)
    load.start()
    load.wait()
    exc = total_ref.shape[0] // 2
    rows = expansion_ref.shape[2]
    columns = tile_of(rows, 768)
    stores = []
    for step in range(rows // columns):
        span = slice(step * columns, (step + 1) * columns)
        first = jnp.dot(total_ref[...], expansion_ref[0, :, span], preferred_element_type=jnp.float32)
        second = jnp.dot(total_ref[...], expansion_ref[1, :, span], preferred_element_type=jnp.float32)
        out[0, :, span] = (first[:exc] - second[exc:]).astype(out.dtype)
        out[1, :, span] = (second[:exc] + first[exc:]).astype(out.dtype)
        at = pl.ds(step * columns, columns)
        store = pltpu.make_async_copy(out.at[:, :, at], out_hbm.at[:, :, at], store_sem.at[step])
        store.start()
        stores.append(store)
    for store in stores:
        store.wait()


def per_device(excitation, point_order, projection, transfer, expansion):
    panels = lax.axis_size("panel")
    levels = transfer.shape[0]
    _, exc, rows = excitation.shape
    rank = projection.shape[1]
    wide = 2 * exc // CHUNKS
    piece = rank // panels
    total = pl.pallas_call(
        functools.partial(coefficients_kernel, panels, levels),
        out_shape=jax.ShapeDtypeStruct((2 * exc, rank), jnp.bfloat16),
        in_specs=[pl.BlockSpec(memory_space=pl.ANY)] * 4,
        out_specs=pl.BlockSpec(memory_space=pltpu.VMEM),
        scratch_shapes=[
            pltpu.VMEM((2 * exc, rows), jnp.bfloat16),
            pltpu.VMEM((1, rows), jnp.int32),
            pltpu.VMEM(projection.shape, jnp.bfloat16),
            pltpu.VMEM(transfer.shape, jnp.bfloat16),
            pltpu.VMEM((2, rank, rank), jnp.bfloat16),
            pltpu.VMEM((rows, 2 * exc), jnp.bfloat16),
            pltpu.VMEM((rows, 128), jnp.int16),
            pltpu.VMEM((rows, 2 * exc), jnp.bfloat16),
            pltpu.VMEM((levels, CHUNKS, rank, wide), jnp.bfloat16),
            pltpu.VMEM((levels, CHUNKS, rank, wide), jnp.bfloat16),
            pltpu.VMEM((CHUNKS, 2, rank, wide), jnp.bfloat16),
            pltpu.VMEM((panels - 1, CHUNKS, 2, piece, wide), jnp.bfloat16),
            pltpu.VMEM((CHUNKS, piece, wide), jnp.bfloat16),
            pltpu.VMEM((CHUNKS, piece, wide), jnp.bfloat16),
            pltpu.VMEM((CHUNKS, rank, wide), jnp.bfloat16),
            pltpu.SemaphoreType.DMA((3 + 2 * CHUNKS,)),
            pltpu.SemaphoreType.DMA((2,)),
            pltpu.SemaphoreType.DMA((levels, CHUNKS)),
            pltpu.SemaphoreType.DMA((levels, CHUNKS)),
            pltpu.SemaphoreType.DMA((panels - 1, CHUNKS)),
            pltpu.SemaphoreType.DMA((panels - 1, CHUNKS)),
            pltpu.SemaphoreType.DMA((CHUNKS,)),
            pltpu.SemaphoreType.DMA((CHUNKS,)),
            pltpu.SemaphoreType.DMA((panels - 1, CHUNKS)),
            pltpu.SemaphoreType.DMA((panels - 1, CHUNKS)),
        ],
        compiler_params=pltpu.CompilerParams(
            collective_id=0, has_side_effects=True, vmem_limit_bytes=60 * MIB
        ),
    )(excitation, point_order, projection, transfer)
    return pl.pallas_call(
        expansion_kernel,
        out_shape=jax.ShapeDtypeStruct((2, exc, rows), jnp.bfloat16),
        in_specs=[pl.BlockSpec(memory_space=pl.ANY), pl.BlockSpec(memory_space=pltpu.VMEM)],
        out_specs=pl.BlockSpec(memory_space=pl.ANY),
        scratch_shapes=[
            pltpu.VMEM((2 * exc, rank), jnp.bfloat16),
            pltpu.VMEM((2, exc, rows), jnp.bfloat16),
            pltpu.SemaphoreType.DMA,
            pltpu.SemaphoreType.DMA((rows // tile_of(rows, 768),)),
        ],
        compiler_params=pltpu.CompilerParams(vmem_limit_bytes=24 * MIB),
    )(total, expansion)


def solution(mesh):
    in_specs = (
        P(None, None, ("panel", "leaf")),
        P(("panel", "leaf"), None),
        P(None, None, ("panel", "leaf")),
        P(None, None, ("panel", "leaf"), None),
        P(None, None, ("panel", "leaf")),
    )
    out_specs = P(None, None, ("panel", "leaf"))
    return jax.shard_map(
        per_device, mesh=mesh, in_specs=in_specs, out_specs=out_specs, check_vma=False
    )
```
